32 devices in a mesh: groups: 2 (over y), tile: 16 (over z, x, core).
Axes of the slice: x: 2, y: 2, z: 4, core: 2. Of those that a mesh axis runs over, the one named last changes fastest.
Arguments:
- params: float32 [10, 32, 16, 256], P('groups', 'tile'), parts along dimension 0, may hold values from 0.5 to 4, as said below
- adjoint_state: float32 [16, 2, 9, 8, 16, 256], P('tile', 'groups'), parts along dimension 1, may hold values from -6 to 6
- snapshots: bfloat16 [16, 2, 6, 3, 8, 16, 256], P('tile', 'groups'), parts along dimension 1, may hold values from -6 to 6
- residuals: float32 [16, 2, 6, 256], P('tile', 'groups'), parts along dimension 1, may hold values from -6 to 6
- receivers: int32 [16, 2, 256], P('tile', 'groups'), parts along dimension 1, may hold values from 0 to 32767
- sources: int32 [16, 2], P('tile', 'groups'), parts along dimension 1, may hold values from 0 to 32767
- offsets: int32 [16], P('tile'), may hold values from 0 to 12, as said below
Outputs:
- gradient: float32 [10, 32, 16, 256], P('groups', 'tile'), parts along dimension 0
The draws below stay inside these ranges and needn't reach their ends.
There are 2 independent parts, one for each index of `groups`. The reference program is written for one: setup_inputs(seed, part) draws one part's arguments, and reference() takes and returns one part's arrays. A program takes and returns all parts, laid end to end along the dimension named above; an argument that names none is the same for every part. Nothing has to cross between parts.
Inputs may be any that keep to these rules, and one draw needn't show every extreme that they name: Shot group g's aperture starts at slab offsets[g], with max(0, g - 3) <= offsets[g] <= min(12, g). params holds buoyancy within 0.5 to 1.0, c11 within 2 to 4, c13 within 0.5 to 1.5, c33 within 2 to 4 and c44 within 0.5 to 1.5.
All inputs are finite; a program needn't handle non-finite values. Where the reference program divides by a largest or mean magnitude, that divisor is 1e-20 or more.
Results may differ from the reference program's by a relative error of at most 0.0003.
Values sent between devices are 32-bit elements; how exact they have to be, the bound alone decides.
A program may use at most 64 MiB of HBM per device.

```python
import jax
import jax.numpy as jnp
from jax import lax

CX = 2
NY = 16
NZ = 256
SHOTS = 1
STEPS = 6
APER = 4
REACH = 3
NREC = 256
MUTE = 4
GROUPS = 16
NX = 32
ACX = 8


def draw_params(key, part):
    unit = jax.random.uniform(key, (5, NX, NY, NZ), jnp.float32)
    lower = jnp.array([0.5, 2.0, 0.5, 2.0, 0.5], jnp.float32).reshape(5, 1, 1, 1)
    upper = jnp.array([1.0, 4.0, 1.5, 4.0, 1.5], jnp.float32).reshape(5, 1, 1, 1)
    return (lower + (upper - lower) * unit).astype(jnp.float32)


def draw_offsets(key, part):
    jitter = jax.random.randint(jax.random.fold_in(key, 17), (GROUPS,), 0, 2 * REACH + 2 - APER)
    start = jnp.arange(GROUPS, dtype=jnp.int32) - REACH + jitter
    return jnp.clip(start, 0, GROUPS - APER).astype(jnp.int32)


def set_ends(drawn, own_key, least, high):
    index_at = [jax.random.randint(jax.random.fold_in(own_key, axis), (), 0, length) for axis, length in enumerate(drawn.shape)]
    longest = drawn.shape.index(max(drawn.shape))
    next_to = index_at[:longest] + [(index_at[longest] + 1) % drawn.shape[longest]] + index_at[longest + 1:]
    return drawn.at[tuple(index_at)].set(least).at[tuple(next_to)].set(high)


def levels(rng, shape, shards, least, top_value):
    loudness, own = 1.0, jax.random.fold_in(rng, 6)
    for position, blocks in shards:
        draws = jnp.exp(jax.random.uniform(jax.random.fold_in(own, position), (blocks,), jnp.float32, least / len(shards), top_value / len(shards)))
        loudness = loudness * jnp.repeat(draws, shape[position] // blocks).reshape([-1 if axis == position else 1 for axis in range(len(shape))])
    return loudness


def scatter_about(stream_key, shape, scale, limit, shards=(), held_as=jnp.bfloat16):
    values = scale * jax.random.normal(stream_key, shape, jnp.float32)
    if shards:
        values = values * levels(stream_key, shape, shards, -0.22, 0.18)
    return jnp.clip(values, -limit, limit).astype(held_as)


def setup_inputs(seed: int = 0, part: int = 0) -> dict:
    arg_keys = jax.random.split(jax.random.key(seed), 8)
    part_keys = jax.random.split(jax.random.fold_in(arg_keys[7], part), 8)
    return {
        "params": draw_params(jax.random.fold_in(jax.random.fold_in(arg_keys[7], part), 71), part),
        "adjoint_state": scatter_about(part_keys[1], (GROUPS, SHOTS, 9, ACX, NY, NZ), 1.0, 6.0, ((0, 16),), jnp.float32),
        "snapshots": scatter_about(part_keys[2], (GROUPS, SHOTS, STEPS, 3, ACX, NY, NZ), 1.0, 6.0, ((0, 16),)),
        "residuals": scatter_about(part_keys[3], (GROUPS, SHOTS, STEPS, NREC), 1.0, 6.0, ((0, 16),), jnp.float32),
        "receivers": set_ends(jax.random.randint(part_keys[4], (GROUPS, SHOTS, NREC), 0, ACX * NY * NZ), jax.random.fold_in(part_keys[4], 1), 0, (ACX * NY * NZ) - 1).astype(jnp.int32),
        "sources": set_ends(jax.random.randint(part_keys[5], (GROUPS, SHOTS), 0, ACX * NY * NZ), jax.random.fold_in(part_keys[5], 1), 0, (ACX * NY * NZ) - 1).astype(jnp.int32),
        "offsets": draw_offsets(jax.random.fold_in(arg_keys[7], 71), part),
    }


STEP_H = 0.2
EPSILON = 1e-6


def forward_diff(wavefield, along):
    length = wavefield.shape[along]
    shifted = lax.slice_in_dim(wavefield, 1, length, axis=along)
    border = jnp.zeros_like(lax.slice_in_dim(wavefield, 0, 1, axis=along))
    return jnp.concatenate([shifted, border], axis=along) - wavefield


def backward_diff(wavefield, along):
    length = wavefield.shape[along]
    behind = lax.slice_in_dim(wavefield, 0, length - 1, axis=along)
    border = jnp.zeros_like(lax.slice_in_dim(wavefield, 0, 1, axis=along))
    return wavefield - jnp.concatenate([border, behind], axis=along)


def strains(velocity_x, velocity_y, velocity_z):
    strain_xx = backward_diff(velocity_x, 0)
    strain_yy = backward_diff(velocity_y, 1)
    strain_zz = backward_diff(velocity_z, 2)
    strain_xy = forward_diff(velocity_x, 1) + forward_diff(velocity_y, 0)
    strain_xz = forward_diff(velocity_x, 2) + forward_diff(velocity_z, 0)
    strain_yz = forward_diff(velocity_y, 2) + forward_diff(velocity_z, 1)
    return strain_xx, strain_yy, strain_zz, strain_xy, strain_xz, strain_yz


def mute_weight(source, grid_shape):
    plane_cells = grid_shape[1] * grid_shape[2]
    source_x = (source // plane_cells).astype(jnp.float32)
    source_y = ((source // grid_shape[2]) % grid_shape[1]).astype(jnp.float32)
    source_z = (source % grid_shape[2]).astype(jnp.float32)
    delta_x = lax.broadcasted_iota(jnp.float32, grid_shape, 0) - source_x
    delta_y = lax.broadcasted_iota(jnp.float32, grid_shape, 1) - source_y
    delta_z = lax.broadcasted_iota(jnp.float32, grid_shape, 2) - source_z
    distance = delta_x * delta_x + delta_y * delta_y + delta_z * delta_z
    return distance / (distance + float(MUTE * MUTE))


def shot_gradient(aperture, adjoint, snapshot, residual, receiver, source):
    buoyancy, stiff_11, stiff_13, stiff_33, stiff_44 = aperture[0], aperture[1], aperture[2], aperture[3], aperture[4]
    stiff_66 = 0.5 * (stiff_11 - stiff_13)
    velocity_x, velocity_y, velocity_z = adjoint[0], adjoint[1], adjoint[2]
    stress_xx, stress_yy, stress_zz = adjoint[3], adjoint[4], adjoint[5]
    stress_xy, stress_xz, stress_yz = adjoint[6], adjoint[7], adjoint[8]
    grid_shape = velocity_x.shape
    kernel_b = jnp.zeros(grid_shape, jnp.float32)
    kernel_11 = jnp.zeros(grid_shape, jnp.float32)
    kernel_13 = jnp.zeros(grid_shape, jnp.float32)
    kernel_33 = jnp.zeros(grid_shape, jnp.float32)
    kernel_44 = jnp.zeros(grid_shape, jnp.float32)
    for step_index in range(STEPS):
        velocity_x = velocity_x + STEP_H * buoyancy * (forward_diff(stress_xx, 0) + backward_diff(stress_xy, 1) + backward_diff(stress_xz, 2))
        velocity_y = velocity_y + STEP_H * buoyancy * (backward_diff(stress_xy, 0) + forward_diff(stress_yy, 1) + backward_diff(stress_yz, 2))
        velocity_z = velocity_z + STEP_H * buoyancy * (backward_diff(stress_xz, 0) + backward_diff(stress_yz, 1) + forward_diff(stress_zz, 2))
        velocity_z = velocity_z.reshape(-1).at[receiver].add(residual[step_index]).reshape(grid_shape)
        strain_xx, strain_yy, strain_zz, strain_xy, strain_xz, strain_yz = strains(velocity_x, velocity_y, velocity_z)
        stress_xx = stress_xx + STEP_H * (stiff_11 * strain_xx + stiff_13 * (strain_yy + strain_zz))
        stress_yy = stress_yy + STEP_H * (stiff_11 * strain_yy + stiff_13 * (strain_xx + strain_zz))
        stress_zz = stress_zz + STEP_H * (stiff_13 * (strain_xx + strain_yy) + stiff_33 * strain_zz)
        stress_xy = stress_xy + STEP_H * stiff_66 * strain_xy
        stress_xz = stress_xz + STEP_H * stiff_44 * strain_xz
        stress_yz = stress_yz + STEP_H * stiff_44 * strain_yz
        forward_x = snapshot[step_index, 0].astype(jnp.float32)
        forward_y = snapshot[step_index, 1].astype(jnp.float32)
        forward_z = snapshot[step_index, 2].astype(jnp.float32)
        forward_xx, forward_yy, forward_zz, forward_xy, forward_xz, forward_yz = strains(forward_x, forward_y, forward_z)
        kernel_b = kernel_b + velocity_x * forward_x + velocity_y * forward_y + velocity_z * forward_z
        kernel_11 = kernel_11 + strain_xx * forward_xx + strain_yy * forward_yy + 0.5 * strain_xy * forward_xy
        kernel_13 = kernel_13 + strain_xx * (forward_yy + forward_zz) + strain_yy * (forward_xx + forward_zz) + strain_zz * (forward_xx + forward_yy) - 0.5 * strain_xy * forward_xy
        kernel_33 = kernel_33 + strain_zz * forward_zz
        kernel_44 = kernel_44 + strain_xz * forward_xz + strain_yz * forward_yz
    weight = mute_weight(source, grid_shape)
    return jnp.stack([kernel_b, kernel_11, kernel_13, kernel_33, kernel_44]) * weight


def reference(params, adjoint_state, snapshots, residuals, receivers, sources, offsets):
    def one_group(summed, inputs):
        adjoint_group, snapshot_group, residual_group, receiver_group, source_group, offset_group = inputs
        start = (offset_group * CX).astype(jnp.int32)
        aperture = lax.dynamic_slice_in_dim(params, start, APER * CX, axis=1)
        contrib = shot_gradient(aperture, adjoint_group[0], snapshot_group[0], residual_group[0], receiver_group[0], source_group[0])
        for shot_index in range(1, SHOTS):
            contrib = contrib + shot_gradient(aperture, adjoint_group[shot_index], snapshot_group[shot_index], residual_group[shot_index], receiver_group[shot_index], source_group[shot_index])
        current = lax.dynamic_slice_in_dim(summed, start, APER * CX, axis=1)
        summed = lax.dynamic_update_slice_in_dim(summed, current + contrib, start, axis=1)
        return summed, None

    summed = jnp.zeros(params.shape, jnp.float32)
    summed, _ = lax.scan(one_group, summed, (adjoint_state, snapshots, residuals, receivers, sources, offsets))
    largest = jnp.max(jnp.abs(summed), axis=(1, 2, 3), keepdims=True)
    return summed / (largest + EPSILON)
```

```python
import functools

import jax
import jax.numpy as jnp
from jax import lax
from jax.experimental import pallas as pl
from jax.experimental.pallas import tpu as pltpu
from jax.sharding import PartitionSpec as P

STEPS = 6
APER = 4
REACH = 3
MUTE = 4
SPAN = 2 * REACH + 1

STEP_H = 0.2
EPSILON = 1e-06
MESH = pl.DeviceIdType.MESH


def shift_up(plane, axis):
    size = plane.shape[axis]
    place = lax.broadcasted_iota(jnp.int32, plane.shape, axis)
    return jnp.where(place == size - 1, 0.0, pltpu.roll(plane, size - 1, axis))


def shift_down(plane, axis):
    place = lax.broadcasted_iota(jnp.int32, plane.shape, axis)
    return jnp.where(place == 0, 0.0, pltpu.roll(plane, 1, axis))


def fwd(plane, axis):
    return shift_up(plane, axis) - plane


def bwd(plane, axis):
    return plane - shift_down(plane, axis)


def strains_at(here, before, after):
    vx, vy, vz = here
    exx = vx if before is None else vx - before
    eyy = bwd(vy, 0)
    ezz = bwd(vz, 1)
    if after is None:
        exy = fwd(vx, 0) - vy
        exz = fwd(vx, 1) - vz
    else:
        exy = fwd(vx, 0) + (after[0] - vy)
        exz = fwd(vx, 1) + (after[1] - vz)
    eyz = fwd(vy, 1) + fwd(vz, 0)
    return exx, eyy, ezz, exy, exz, eyz


def kernel(
    tiles,
    offsets,
    sources,
    params,
    adjoint,
    snapshots,
    residuals,
    receivers,
    out,
    window,
    state,
    snaps,
    inject,
    fstrain,
    coef,
    grad,
    gwin,
    fromp,
    sumbuf,
    landed,
    mine,
    maxima,
    local_sem,
    p_send,
    p_recv,
    g_send,
    g_recv,
    m_send,
    m_recv,
):
    me = lax.axis_index("tile")
    core = lax.rem(me, 2)
    partner = me + 1 - 2 * core
    far = me + 3 * (2 * core - 1)
    nx = state.shape[1]
    slab = params.shape[1]
    ny, nz = state.shape[2], state.shape[3]

    own_copy = pltpu.make_async_copy(params, window.at[REACH], local_sem.at[0])
    state_copy = pltpu.make_async_copy(adjoint.at[0, 0], state, local_sem.at[1])
    snap_copy = pltpu.make_async_copy(snapshots.at[0, 0], snaps, local_sem.at[2])
    own_copy.start()
    snap_copy.start()
    state_copy.start()

    barrier = pltpu.get_barrier_semaphore()

    @pl.loop(1, tiles)
    def _(d):
        pl.semaphore_signal(
            barrier, inc=1, device_id={"tile": lax.rem(me + d, tiles)}, device_id_type=MESH
        )

    pl.semaphore_wait(barrier, tiles - 1)

    def inside(t):
        return jnp.logical_and(t >= 0, t < tiles)

    def push(src, dst, sems, recvs, s, r, to):
        return pltpu.make_async_remote_copy(
            src_ref=src,
            dst_ref=dst,
            send_sem=sems.at[s],
            recv_sem=recvs.at[r],
            device_id={"tile": to},
            device_id_type=MESH,
        )

    def when_in(t, fn):
        pl.when(inside(t))(fn)

    send_far = push(params, window.at[6 * (1 - core)], p_send, p_recv, 0, 6 * (1 - core), far)
    send_up = push(params, window.at[1], p_send, p_recv, 1, 1, me + 2)
    send_dn = push(params, window.at[5], p_send, p_recv, 2, 5, me - 2)
    send_pa = push(params, window.at[2 + 2 * core], p_send, p_recv, 3, 2 + 2 * core, partner)
    when_in(me + 2, send_up.start)
    when_in(me - 2, send_dn.start)
    when_in(far, send_far.start)
    send_pa.start()

    cells = receivers[...]
    lanes = cells.shape[1]
    rows = nx * ny
    row_of = lax.div(cells, nz)
    col_of = lax.rem(cells, nz)
    row_hit = lax.broadcasted_iota(jnp.int32, (rows, lanes), 0) == row_of
    col_hit = lax.broadcasted_iota(jnp.int32, (nz, lanes), 0) == col_of
    columns = jnp.where(col_hit, 1.0, 0.0).astype(jnp.bfloat16)
    for s in range(STEPS):
        rest = residuals[0, 0, s : s + 1, :]
        total = None
        for part in range(3):
            piece = rest.astype(jnp.bfloat16).astype(jnp.float32)
            rest = rest - piece
            left = jnp.where(row_hit, piece, 0.0).astype(jnp.bfloat16)
            term = lax.dot_general(
                left, columns, (((1,), (1,)), ((), ())), preferred_element_type=jnp.float32
            )
            total = term if total is None else total + term
        inject[s] = total.reshape(nx, ny, nz)

    snap_copy.wait()

    @pl.loop(0, STEPS)
    def _(s):
        u = [[snaps[s, c, i].astype(jnp.float32) for i in range(nx)] for c in range(3)]
        for i in range(nx):
            here = (u[0][i], u[1][i], u[2][i])
            before = u[0][i - 1] if i > 0 else None
            after = (u[1][i + 1], u[2][i + 1]) if i + 1 < nx else None
            f = strains_at(here, before, after)
            for k in range(6):
                fstrain[s, k, i] = 0.5 * f[k] if k == 3 else f[k]

    relay_up = push(window.at[5], window.at[4 + 2 * core], p_send, p_recv, 4, 4 + 2 * core, partner)
    relay_dn = push(window.at[1], window.at[2 * core], p_send, p_recv, 5, 2 * core, partner)

    def arrived(slot):
        push(params, window.at[slot], p_send, p_recv, 0, slot, partner).wait_recv()

    def pass_up():
        arrived(5)
        relay_up.start()

    def pass_dn():
        arrived(1)
        relay_dn.start()

    when_in(me + 2, pass_up)
    when_in(me - 2, pass_dn)
    for slot in (0, 2, 4, 6):
        when_in(me + slot - REACH, functools.partial(arrived, slot))
    own_copy.wait()
    state_copy.wait()

    rel = jnp.clip(offsets[0] - me + REACH, 0, REACH)
    for j in range(APER):
        b, c11, c13, c33, c44 = [window[rel + j, f] for f in range(5)]
        here = slice(j * slab, (j + 1) * slab)
        coef[0, here] = STEP_H * b
        coef[1, here] = STEP_H * c11
        coef[2, here] = STEP_H * c13
        coef[3, here] = STEP_H * c33
        coef[4, here] = STEP_H * c44
        coef[5, here] = (0.5 * STEP_H) * (c11 - c13)

    grad[...] = jnp.zeros_like(grad)

    @pl.loop(0, STEPS)
    def _(s):
        def velocity(i):
            hb = coef[0, i]
            sxx, syy, szz, sxy, sxz, syz = [state[3 + k, i] for k in range(6)]
            dxx = state[3, i + 1] - sxx if i + 1 < nx else -sxx
            dxy = sxy - state[6, i - 1] if i > 0 else sxy
            dxz = sxz - state[7, i - 1] if i > 0 else sxz
            vx = state[0, i] + hb * (dxx + bwd(sxy, 0) + bwd(sxz, 1))
            vy = state[1, i] + hb * (dxy + fwd(syy, 0) + bwd(syz, 1))
            vz = state[2, i] + hb * (dxz + bwd(syz, 0) + fwd(szz, 1)) + inject[s, i]
            state[0, i] = vx
            state[1, i] = vy
            state[2, i] = vz
            return vx, vy, vz

        def stress(i, before, here, after):
            vx, vy, vz = here
            exx, eyy, ezz, exy, exz, eyz = strains_at(
                here, None if before is None else before[0], None if after is None else after[1:]
            )
            h11, h13, h33, h44, h66 = [coef[k, i] for k in range(1, 6)]
            state[3, i] = state[3, i] + (h11 * exx + h13 * (eyy + ezz))
            state[4, i] = state[4, i] + (h11 * eyy + h13 * (exx + ezz))
            state[5, i] = state[5, i] + (h13 * (exx + eyy) + h33 * ezz)
            state[6, i] = state[6, i] + h66 * exy
            state[7, i] = state[7, i] + h44 * exz
            state[8, i] = state[8, i] + h44 * eyz
            fxx, fyy, fzz, fxy, fxz, fyz = [fstrain[s, k, i] for k in range(6)]
            ux, uy, uz = [snaps[s, c, i].astype(jnp.float32) for c in range(3)]
            shear = exy * fxy
            grad[0, i] = grad[0, i] + (vx * ux + vy * uy + vz * uz)
            grad[1, i] = grad[1, i] + (exx * fxx + eyy * fyy + shear)
            grad[2, i] = grad[2, i] + (
                exx * (fyy + fzz) + eyy * (fxx + fzz) + ezz * (fxx + fyy) - shear
            )
            grad[3, i] = grad[3, i] + ezz * fzz
            grad[4, i] = grad[4, i] + (exz * fxz + eyz * fyz)

        before, here = None, velocity(0)
        for i in range(nx):
            after = velocity(i + 1) if i + 1 < nx else None
            stress(i, before, here, after)
            before, here = here, after

    source = sources[0, 0]
    sx = lax.div(source, ny * nz)
    sy = lax.rem(lax.div(source, nz), ny)
    sz = lax.rem(source, nz)
    dy = lax.broadcasted_iota(jnp.int32, (ny, nz), 0) - sy
    dz = lax.broadcasted_iota(jnp.int32, (ny, nz), 1) - sz
    flat = dy * dy + dz * dz
    for i in range(nx):
        dx = i - sx
        d2 = (flat + dx * dx).astype(jnp.float32)
        weight = d2 / (d2 + float(MUTE * MUTE))
        for f in range(5):
            grad[f, i] = grad[f, i] * weight

    def place(pos):
        j = pos - rel
        ok = jnp.logical_and(j >= 0, j < APER)
        start = slab * jnp.clip(j, 0, APER - 1)
        for f in range(5):
            for k in range(slab):
                gwin[pos, f, k] = jnp.where(ok, grad[f, start + k], 0.0)

    for pos in range(SPAN):
        place(pos)

    to_pair = [
        push(gwin.at[2 * (1 - core) + 2 * j], fromp.at[j], g_send, g_recv, j, j, partner)
        for j in range(3)
    ]
    to_far = push(gwin.at[6 * core], landed.at[2], g_send, g_recv, 3, 5, far)
    when_in(far, to_far.start)
    for j in (2, 0, 1):
        to_pair[j].start()
    to_up = push(sumbuf.at[0], landed.at[0], g_send, g_recv, 4, 3, me + 2)
    to_dn = push(sumbuf.at[1], landed.at[1], g_send, g_recv, 5, 4, me - 2)
    to_pair[2].wait_recv()
    sumbuf[0] = gwin[5] + fromp[2]
    when_in(me + 2, to_up.start)
    to_pair[0].wait_recv()
    sumbuf[1] = gwin[1] + fromp[0]
    when_in(me - 2, to_dn.start)
    to_pair[1].wait_recv()
    out[...] = gwin[REACH] + fromp[1]

    def add_landed(k, sem):
        def go():
            push(sumbuf.at[0], landed.at[k], g_send, g_recv, 0, sem, partner).wait_recv()
            out[...] += landed[k]

        return go

    when_in(me - 2, add_landed(0, 3))
    when_in(me + 2, add_landed(1, 4))
    when_in(far, add_landed(2, 5))

    for f in range(5):
        biggest = jnp.max(jnp.abs(out[f]))
        mine[f : f + 1, :] = jnp.full((1, 128), biggest, jnp.float32)
    mine[5:8, :] = jnp.zeros((3, 128), jnp.float32)

    def max_copy(d):
        to = lax.rem(me + d, tiles)
        return push(mine, maxima.at[d - 1], m_send, m_recv, d - 1, d - 1, to)

    @pl.loop(1, tiles)
    def _(d):
        max_copy(d).start()

    def take(d, largest):
        max_copy(d).wait_recv()
        return jnp.maximum(largest, maxima[d - 1])

    largest = lax.fori_loop(1, tiles, take, mine[...])
    scale = 1.0 / (largest + EPSILON)
    for f in range(5):
        row = jnp.concatenate([scale[f : f + 1, :]] * (nz // 128), axis=1)
        out[f] = out[f] * row

    when_in(me + 2, send_up.wait_send)
    when_in(me - 2, send_dn.wait_send)
    when_in(far, send_far.wait_send)
    send_pa.wait_send()
    when_in(me + 2, relay_up.wait_send)
    when_in(me - 2, relay_dn.wait_send)
    for j in range(3):
        to_pair[j].wait_send()
    when_in(far, to_far.wait_send)
    when_in(me + 2, to_up.wait_send)
    when_in(me - 2, to_dn.wait_send)

    @pl.loop(1, tiles)
    def _(d):
        max_copy(d).wait_send()


def on_device(params, adjoint_state, snapshots, residuals, receivers, sources, offsets):
    tiles = lax.axis_size("tile")
    grid = adjoint_state.shape[3:]
    slab_shape = params.shape
    f32 = jnp.float32
    any_spec = pl.BlockSpec(memory_space=pl.ANY)
    smem = pl.BlockSpec(memory_space=pltpu.SMEM)
    vmem = pl.BlockSpec(memory_space=pltpu.VMEM)
    dma = pltpu.SemaphoreType.DMA
    return pl.pallas_call(
        functools.partial(kernel, tiles),
        out_shape=jax.ShapeDtypeStruct(slab_shape, f32),
        in_specs=[smem, smem, any_spec, any_spec, any_spec, vmem, vmem],
        out_specs=vmem,
        scratch_shapes=[
            pltpu.VMEM((SPAN,) + slab_shape, f32),
            pltpu.VMEM((9,) + grid, f32),
            pltpu.VMEM((STEPS, 3) + grid, jnp.bfloat16),
            pltpu.VMEM((STEPS,) + grid, f32),
            pltpu.VMEM((STEPS, 6) + grid, f32),
            pltpu.VMEM((6,) + grid, f32),
            pltpu.VMEM((5,) + grid, f32),
            pltpu.VMEM((SPAN,) + slab_shape, f32),
            pltpu.VMEM((3,) + slab_shape, f32),
            pltpu.VMEM((2,) + slab_shape, f32),
            pltpu.VMEM((3,) + slab_shape, f32),
            pltpu.VMEM((8, 128), f32),
            pltpu.VMEM((tiles - 1, 8, 128), f32),
            dma((3,)),
            dma((6,)),
            dma((SPAN,)),
            dma((6,)),
            dma((6,)),
            dma((tiles - 1,)),
            dma((tiles - 1,)),
        ],
        compiler_params=pltpu.CompilerParams(
            collective_id=0, has_side_effects=True, vmem_limit_bytes=40 * 1024 * 1024
        ),
    )(offsets, sources, params, adjoint_state, snapshots, residuals, receivers[0])


def solution(mesh):
    placed = (
        P("groups", "tile", None, None),
        P("tile", "groups", None, None, None, None),
        P("tile", "groups", None, None, None, None, None),
        P("tile", "groups", None, None),
        P("tile", "groups", None),
        P("tile", "groups"),
        P("tile"),
    )
    return jax.shard_map(
        on_device,
        mesh=mesh,
        in_specs=placed,
        out_specs=P("groups", "tile", None, None),
        check_vma=False,
    )
```

```python
import functools

import jax
import jax.numpy as jnp
from jax import lax
from jax.experimental import pallas as pl
from jax.experimental.pallas import tpu as pltpu
from jax.sharding import PartitionSpec as P

STEPS = 6
APER = 4
REACH = 3
MUTE = 4
SPAN = 2 * REACH + 1

STEP_H = 0.2
EPSILON = 1e-06
MESH = pl.DeviceIdType.MESH


def shift(blocks, axis, by):
    rows, columns = len(blocks), len(blocks[0])
    size = blocks[0][0].shape[axis]
    place = lax.broadcasted_iota(jnp.int32, blocks[0][0].shape, axis)
    edge = place == (size - 1 if by == 1 else 0)
    turn = size - 1 if by == 1 else 1
    rolled = [[pltpu.roll(b, turn, axis) for b in row] for row in blocks]

    def beyond(r, c):
        if axis == 0:
            r += by
        else:
            c += by
        return rolled[r][c] if 0 <= r < rows and 0 <= c < columns else 0.0

    return [
        [jnp.where(edge, beyond(r, c), rolled[r][c]) for c in range(columns)] for r in range(rows)
    ]


def per_block(fn, *planes):
    return [[fn(*cells) for cells in zip(*rows)] for rows in zip(*planes)]


def add(a, b):
    return per_block(lambda x, y: x + y, a, b)


def sub(a, b):
    return per_block(lambda x, y: x - y, a, b)


def mul(a, b):
    return per_block(lambda x, y: x * y, a, b)


def fwd(plane, axis):
    return sub(shift(plane, axis, 1), plane)


def bwd(plane, axis):
    return sub(plane, shift(plane, axis, -1))


def read(ref, *at):
    ny, nz = ref.shape[-2:]
    return [[ref[(*at, pl.ds(r, 8), pl.ds(c, 128))] for c in range(0, nz, 128)] for r in range(0, ny, 8)]


def write(ref, plane, *at):
    for r, row in enumerate(plane):
        for c, block in enumerate(row):
            ref[(*at, pl.ds(8 * r, 8), pl.ds(128 * c, 128))] = block


def strains_at(here, before, after):
    vx, vy, vz = here
    exx = vx if before is None else sub(vx, before)
    eyy = bwd(vy, 0)
    ezz = bwd(vz, 1)
    if after is None:
        exy = sub(fwd(vx, 0), vy)
        exz = sub(fwd(vx, 1), vz)
    else:
        exy = add(fwd(vx, 0), sub(after[0], vy))
        exz = add(fwd(vx, 1), sub(after[1], vz))
    eyz = add(fwd(vy, 1), fwd(vz, 0))
    return exx, eyy, ezz, exy, exz, eyz


def kernel(
    tiles,
    offsets,
    sources,
    params,
    adjoint,
    snapshots,
    residuals,
    receivers,
    out,
    window,
    state,
    snaps,
    resid,
    recs,
    inject,
    fields,
    coef,
    grad,
    gwin,
    fromp,
    sumbuf,
    landed,
    mine,
    maxima,
    local_sem,
    p_send,
    p_recv,
    g_send,
    g_recv,
    m_send,
    m_recv,
):
    me = lax.axis_index("tile")
    core = lax.rem(me, 2)
    xbit = lax.rem(lax.div(me, 2), 2)
    partner = me + 1 - 2 * core
    far = me + 3 * (2 * core - 1)
    xn = me + 2 - 4 * xbit
    zf = me + 4 - 8 * xbit
    zr = me - 4 + 8 * xbit
    nx = state.shape[1]
    nf, slab = params.shape[:2]
    ny, nz = state.shape[2], state.shape[3]

    barrier = pltpu.get_barrier_semaphore()

    @pl.loop(1, tiles)
    def _(d):
        pl.semaphore_signal(
            barrier, inc=1, device_id={"tile": lax.rem(me + d, tiles)}, device_id_type=MESH
        )

    own_copy = pltpu.make_async_copy(params, window.at[REACH], local_sem.at[0])
    state_copy = pltpu.make_async_copy(adjoint.at[0, 0], state, local_sem.at[1])
    snap_copy = pltpu.make_async_copy(snapshots.at[0, 0], snaps, local_sem.at[2])
    resid_copy = pltpu.make_async_copy(residuals, resid, local_sem.at[3])
    recs_copy = pltpu.make_async_copy(receivers, recs, local_sem.at[4])
    for copy in (recs_copy, resid_copy, snap_copy, own_copy, state_copy):
        copy.start()
    pl.semaphore_wait(barrier, tiles - 1)

    def push(src, dst, send, recv, to):
        return pltpu.make_async_remote_copy(
            src_ref=src,
            dst_ref=dst,
            send_sem=send,
            recv_sem=recv,
            device_id={"tile": to},
            device_id_type=MESH,
        )

    def when_in(t, fn):
        pl.when(jnp.logical_and(t >= 0, t < tiles))(fn)

    slot_x = 5 - 4 * xbit
    slot_z = 1 + 4 * xbit
    to_core = 2 * core - 1

    def send_x(f):
        return push(params.at[f], window.at[slot_z, f], p_send.at[0], p_recv.at[f], xn)

    send_own = push(params, window.at[2 + 2 * core], p_send.at[1], p_recv.at[10], partner)
    send_far = push(params, window.at[6 - 6 * core], p_send.at[2], p_recv.at[11], far)
    for f in range(nf):
        send_x(f).start()
    send_own.start()
    when_in(far, send_far.start)

    def on_z(f):
        block = window.at[slot_x, f]
        return push(block, window.at[slot_z, f], p_send.at[3], p_recv.at[5 + f], zf)

    def relay_x(f):
        block = window.at[slot_x, f]
        return push(block, window.at[slot_x + to_core, f], p_send.at[4], p_recv.at[12], partner)

    def relay_z(f):
        block = window.at[slot_z, f]
        return push(block, window.at[slot_z + to_core, f], p_send.at[5], p_recv.at[13], partner)

    def got(block, sem):
        push(block, block, p_send.at[0], sem, partner).wait_recv()

    def gone(block, sem):
        push(block, block, sem, p_recv.at[0], partner).wait_send()

    recs_copy.wait()
    resid_copy.wait()
    cells = recs[...]
    lanes = cells.shape[1]
    rows = nx * ny
    row_hit = lax.broadcasted_iota(jnp.int32, (rows, lanes), 0) == lax.div(cells, nz)
    col_hit = lax.broadcasted_iota(jnp.int32, (nz, lanes), 0) == lax.rem(cells, nz)
    columns = jnp.where(col_hit, 1.0, 0.0).astype(jnp.bfloat16)
    for s in range(STEPS):
        rest = resid[s]
        total = None
        for part in range(3):
            piece = rest.astype(jnp.bfloat16).astype(jnp.float32)
            rest = rest - piece
            left = jnp.where(row_hit, piece, 0.0).astype(jnp.bfloat16)
            term = lax.dot_general(
                left, columns, (((1,), (1,)), ((), ())), preferred_element_type=jnp.float32
            )
            total = term if total is None else total + term
        inject[s] = total.reshape(nx, ny, nz)

    snap_copy.wait()

    @pl.loop(0, STEPS)
    def _(s):
        @pl.when(s < nf)
        def _():
            got(window.at[slot_x, s], p_recv.at[s])
            when_in(zf, lambda: on_z(s).start())
            relay_x(s).start()

        def velocity(i):
            planes = []
            for c in range(3):
                u = snaps[s, c, i].astype(jnp.float32)
                blocks = [[u[r : r + 8, k : k + 128] for k in range(0, nz, 128)] for r in range(0, ny, 8)]
                planes.append(blocks)
                write(fields, blocks, s, 7 + c, i)
            return planes

        before, here = None, velocity(0)
        for i in range(nx):
            after = velocity(i + 1) if i + 1 < nx else None
            f = strains_at(
                here, None if before is None else before[0], None if after is None else after[1:]
            )
            fxx, fyy, fzz, fxy, fxz, fyz = f
            half = per_block(lambda x: 0.5 * x, fxy)
            trace = add(add(fxx, fyy), fzz)
            for k, plane in enumerate((fxx, fyy, fzz, half, fxz, fyz, trace)):
                write(fields, plane, s, k, i)
            before, here = here, after

    @pl.loop(0, nf)
    def _(f):
        def go():
            got(window.at[slot_z, f], p_recv.at[5 + f])
            relay_z(f).start()

        when_in(zr, go)

    got(window.at[4 - 2 * core], p_recv.at[10])
    when_in(far, lambda: got(window.at[6 * core], p_recv.at[11]))
    got(window.at[slot_x - to_core], p_recv.at[12])
    when_in(zr, lambda: got(window.at[slot_z - to_core], p_recv.at[13]))
    own_copy.wait()
    state_copy.wait()

    rel = jnp.clip(offsets[0] - me + REACH, 0, REACH)
    for j in range(APER):
        b, c11, c13, c33, c44 = [window[rel + j, f] for f in range(5)]
        here = slice(j * slab, (j + 1) * slab)
        coef[0, here] = STEP_H * b
        coef[1, here] = STEP_H * c13
        coef[2, here] = STEP_H * (c11 - c13)
        coef[3, here] = STEP_H * (c33 - c13)
        coef[4, here] = STEP_H * c44
        coef[5, here] = (0.5 * STEP_H) * (c11 - c13)

    grad[...] = jnp.zeros_like(grad)

    @pl.loop(0, STEPS)
    def _(s):
        def velocity(i):
            hb = read(coef, 0, i)
            sxx, syy, szz, sxy, sxz, syz = [read(state, 3 + k, i) for k in range(6)]
            if i + 1 < nx:
                dxx = sub(read(state, 3, i + 1), sxx)
            else:
                dxx = per_block(lambda x: -x, sxx)
            dxy = sub(sxy, read(state, 6, i - 1)) if i > 0 else sxy
            dxz = sub(sxz, read(state, 7, i - 1)) if i > 0 else sxz
            ax = add(dxx, add(bwd(sxy, 0), bwd(sxz, 1)))
            ay = add(dxy, add(fwd(syy, 0), bwd(syz, 1)))
            az = add(dxz, add(bwd(syz, 0), fwd(szz, 1)))
            vx = add(read(state, 0, i), mul(hb, ax))
            vy = add(read(state, 1, i), mul(hb, ay))
            vz = add(add(read(state, 2, i), read(inject, s, i)), mul(hb, az))
            for k, v in enumerate((vx, vy, vz)):
                write(state, v, k, i)

        def grow(ref, plane, *at):
            write(ref, add(read(ref, *at), plane), *at)

        def stress(i):
            here = [read(state, k, i) for k in range(3)]
            vx, vy, vz = here
            exx, eyy, ezz, exy, exz, eyz = strains_at(
                here,
                read(state, 0, i - 1) if i > 0 else None,
                [read(state, k, i + 1) for k in (1, 2)] if i + 1 < nx else None,
            )
            h13, d11, d33, h44, h66 = [read(coef, k, i) for k in range(1, 6)]
            trace = add(add(exx, eyy), ezz)
            common = mul(h13, trace)
            grow(state, add(common, mul(d11, exx)), 3, i)
            grow(state, add(common, mul(d11, eyy)), 4, i)
            grow(state, add(common, mul(d33, ezz)), 5, i)
            grow(state, mul(h66, exy), 6, i)
            grow(state, mul(h44, exz), 7, i)
            grow(state, mul(h44, eyz), 8, i)
            fxx, fyy, fzz, fxy, fxz, fyz, ftrace, ux, uy, uz = [read(fields, s, k, i) for k in range(10)]
            grow(grad, add(add(mul(vx, ux), mul(vy, uy)), mul(vz, uz)), 0, i)
            grow(grad, add(add(mul(exx, fxx), mul(eyy, fyy)), mul(exy, fxy)), 1, i)
            grow(grad, mul(trace, ftrace), 2, i)
            grow(grad, mul(ezz, fzz), 3, i)
            grow(grad, add(mul(exz, fxz), mul(eyz, fyz)), 4, i)

        velocity(0)
        for i in range(nx):
            if i + 1 < nx:
                velocity(i + 1)
            stress(i)

    source = sources[0, 0]
    sx = lax.div(source, ny * nz)
    sy = lax.rem(lax.div(source, nz), ny)
    sz = lax.rem(source, nz)
    dy = lax.broadcasted_iota(jnp.int32, (ny, nz), 0) - sy
    dz = lax.broadcasted_iota(jnp.int32, (ny, nz), 1) - sz
    flat = dy * dy + dz * dz
    for i in range(nx):
        dx = i - sx
        d2 = (flat + dx * dx).astype(jnp.float32)
        weight = d2 / (d2 + float(MUTE * MUTE))
        k11, k33 = grad[1, i], grad[3, i]
        grad[2, i] = (grad[2, i] - k11 - k33) * weight
        grad[1, i] = k11 * weight
        grad[3, i] = k33 * weight
        grad[0, i] = grad[0, i] * weight
        grad[4, i] = grad[4, i] * weight

    def place(pos):
        j = pos - rel
        ok = jnp.logical_and(j >= 0, j < APER)
        start = slab * jnp.clip(j, 0, APER - 1)
        for f in range(5):
            for k in range(slab):
                gwin[pos, f, k] = jnp.where(ok, grad[f, start + k], 0.0)

    pair = [
        push(gwin.at[pos - to_core], fromp.at[k], g_send.at[k], g_recv.at[10 + k], partner)
        for k, pos in enumerate((slot_z, slot_x, REACH))
    ]
    to_far = push(gwin.at[6 * core], landed.at[2], g_send.at[5], g_recv.at[13], far)
    for k, pos in enumerate((slot_z, slot_x, REACH)):
        place(pos - to_core)
        pair[k].start()
    place(slot_z)
    place(6 * core)
    place(slot_x)
    place(REACH)

    def to_z(f):
        return push(sumbuf.at[0, f], landed.at[0, f], g_send.at[3], g_recv.at[5 + f], zr)

    def to_x(f):
        return push(sumbuf.at[1, f], landed.at[1, f], g_send.at[4], g_recv.at[f], xn)

    pair[0].wait_recv()
    for f in range(nf):
        sumbuf[0, f] = gwin[slot_z, f] + fromp[0, f]
        when_in(zr, to_z(f).start)
    when_in(far, to_far.start)
    pair[1].wait_recv()
    for f in range(nf):
        sumbuf[1, f] = gwin[slot_x, f] + fromp[1, f]

        def join(f=f):
            got(landed.at[0, f], g_recv.at[5 + f])
            sumbuf[1, f] += landed[0, f]

        when_in(zf, join)
        to_x(f).start()
    pair[2].wait_recv()
    out[...] = gwin[REACH] + fromp[2]

    def join_far():
        got(landed.at[2], g_recv.at[13])
        out[...] += landed[2]

    when_in(far, join_far)

    for f in range(nf):
        got(landed.at[1, f], g_recv.at[f])
        total = out[f] + landed[1, f]
        out[f] = total
        biggest = jnp.max(jnp.abs(total), axis=(0, 1, 2), keepdims=True)
        mine[f : f + 1, :] = jnp.broadcast_to(biggest[0], (1, 128))
    mine[nf:8, :] = jnp.zeros((8 - nf, 128), jnp.float32)

    def max_copy(d):
        to = lax.rem(me + d, tiles)
        return push(mine, maxima.at[d - 1], m_send.at[d - 1], m_recv.at[d - 1], to)

    @pl.loop(1, tiles)
    def _(d):
        max_copy(d).start()

    gone(params, p_send.at[0])
    send_own.wait_send()
    when_in(far, send_far.wait_send)
    when_in(zf, lambda: gone(window.at[slot_x], p_send.at[3]))
    gone(window.at[slot_x], p_send.at[4])
    when_in(zr, lambda: gone(window.at[slot_z], p_send.at[5]))
    for copy in pair:
        copy.wait_send()
    when_in(far, to_far.wait_send)
    when_in(zr, lambda: gone(sumbuf.at[0], g_send.at[3]))
    gone(sumbuf.at[1], g_send.at[4])

    def take(d, largest):
        max_copy(d).wait_recv()
        return jnp.maximum(largest, maxima[d - 1])

    largest = lax.fori_loop(1, tiles, take, mine[...])
    scale = 1.0 / (largest + EPSILON)
    for f in range(nf):
        row = jnp.concatenate([scale[f : f + 1, :]] * (nz // 128), axis=1)
        out[f] = out[f] * row

    @pl.loop(1, tiles)
    def _(d):
        max_copy(d).wait_send()


def on_device(params, adjoint_state, snapshots, residuals, receivers, sources, offsets):
    tiles = lax.axis_size("tile")
    grid = adjoint_state.shape[3:]
    slab_shape = params.shape
    f32 = jnp.float32
    hbm = pl.BlockSpec(memory_space=pltpu.HBM)
    smem = pl.BlockSpec(memory_space=pltpu.SMEM)
    vmem = pl.BlockSpec(memory_space=pltpu.VMEM)
    dma = pltpu.SemaphoreType.DMA
    rows = jnp.transpose(residuals[0], (1, 0, 2))
    return pl.pallas_call(
        functools.partial(kernel, tiles),
        out_shape=jax.ShapeDtypeStruct(slab_shape, f32),
        in_specs=[smem, smem, hbm, hbm, hbm, hbm, hbm],
        out_specs=vmem,
        scratch_shapes=[
            pltpu.VMEM((SPAN,) + slab_shape, f32),
            pltpu.VMEM((9,) + grid, f32),
            pltpu.VMEM((STEPS, 3) + grid, jnp.bfloat16),
            pltpu.VMEM(rows.shape, f32),
            pltpu.VMEM(receivers.shape[1:], jnp.int32),
            pltpu.VMEM((STEPS,) + grid, f32),
            pltpu.VMEM((STEPS, 10) + grid, f32),
            pltpu.VMEM((6,) + grid, f32),
            pltpu.VMEM((5,) + grid, f32),
            pltpu.VMEM((SPAN,) + slab_shape, f32),
            pltpu.VMEM((3,) + slab_shape, f32),
            pltpu.VMEM((2,) + slab_shape, f32),
            pltpu.VMEM((3,) + slab_shape, f32),
            pltpu.VMEM((8, 128), f32),
            pltpu.VMEM((tiles - 1, 8, 128), f32),
            dma((5,)),
            dma((6,)),
            dma((14,)),
            dma((6,)),
            dma((14,)),
            dma((tiles - 1,)),
            dma((tiles - 1,)),
        ],
        compiler_params=pltpu.CompilerParams(
            collective_id=0, has_side_effects=True, vmem_limit_bytes=56 * 1024 * 1024
        ),
    )(offsets, sources, params, adjoint_state, snapshots, rows, receivers[0])


def solution(mesh):
    placed = (
        P("groups", "tile", None, None),
        P("tile", "groups", None, None, None, None),
        P("tile", "groups", None, None, None, None, None),
        P("tile", "groups", None, None),
        P("tile", "groups", None),
        P("tile", "groups"),
        P("tile"),
    )
    return jax.shard_map(
        on_device,
        mesh=mesh,
        in_specs=placed,
        out_specs=P("groups", "tile", None, None),
        check_vma=False,
    )
```

```python
import functools

import jax
import jax.numpy as jnp
from jax import lax
from jax.experimental import pallas as pl
from jax.experimental.pallas import tpu as pltpu
from jax.sharding import PartitionSpec as P

STEPS = 6
APER = 4
REACH = 3
MUTE = 4
SPAN = 2 * REACH + 1

STEP_H = 0.2
EPSILON = 1e-06
MESH = pl.DeviceIdType.MESH


def shifted(blocks, axis, by):
    rows, columns = len(blocks), len(blocks[0])
    size = blocks[0][0].shape[axis]
    place = lax.broadcasted_iota(jnp.int32, blocks[0][0].shape, axis)
    edge = place == (size - 1 if by == 1 else 0)
    turn = size - 1 if by == 1 else 1
    rolled = [[pltpu.roll(b, turn, axis) for b in row] for row in blocks]

    def at(r, c):
        nr, nc = (r + by, c) if axis == 0 else (r, c + by)
        beyond = rolled[nr][nc] if 0 <= nr < rows and 0 <= nc < columns else 0.0
        return jnp.where(edge, beyond, rolled[r][c])

    return at


def block_of(r, c):
    return pl.ds(8 * r, 8), pl.ds(128 * c, 128)


def read(ref, *at):
    ny, nz = ref.shape[-2:]
    return [[ref[(*at, *block_of(r, c))] for c in range(nz // 128)] for r in range(ny // 8)]


def strains_of(here, before, after):
    vx, vy, vz = here
    vx_y, vx_z = shifted(vx, 0, 1), shifted(vx, 1, 1)
    vy_y, vy_z = shifted(vy, 0, -1), shifted(vy, 1, 1)
    vz_y, vz_z = shifted(vz, 0, 1), shifted(vz, 1, -1)

    def at(r, c):
        x, y, z = vx[r][c], vy[r][c], vz[r][c]
        exx = x if before is None else x - before(r, c)
        eyy = y - vy_y(r, c)
        ezz = z - vz_z(r, c)
        dy = -y if after is None else after[0](r, c) - y
        dz = -z if after is None else after[1](r, c) - z
        exy = (vx_y(r, c) - x) + dy
        exz = (vx_z(r, c) - x) + dz
        eyz = (vy_z(r, c) - y) + (vz_y(r, c) - z)
        return exx, eyy, ezz, exy, exz, eyz

    return at


def kernel(
    tiles,
    offsets,
    sources,
    params,
    adjoint,
    snapshots,
    residuals,
    receivers,
    summed,
    scales,
    out,
    offset,
    source_at,
    window,
    state,
    snaps,
    resid,
    recs,
    inject,
    fields,
    coef,
    grad,
    gwin,
    fromp,
    sumbuf,
    landed,
    mine,
    maxima,
    local_sem,
    p_send,
    p_recv,
    g_send,
    g_recv,
    m_send,
    m_recv,
):
    me = lax.axis_index("tile")
    core = lax.rem(me, 2)
    xbit = lax.rem(lax.div(me, 2), 2)
    partner = me + 1 - 2 * core
    far = me + 3 * (2 * core - 1)
    xn = me + 2 - 4 * xbit
    zf = me + 4 - 8 * xbit
    zr = me - 4 + 8 * xbit
    nx = state.shape[1]
    nf, slab = params.shape[:2]
    ny, nz = state.shape[2], state.shape[3]

    barrier = pltpu.get_barrier_semaphore()

    @pl.loop(1, tiles)
    def _(d):
        pl.semaphore_signal(
            barrier, inc=1, device_id={"tile": lax.rem(me + d, tiles)}, device_id_type=MESH
        )

    own_copy = pltpu.make_async_copy(params, window.at[REACH], local_sem.at[0])
    state_copy = pltpu.make_async_copy(adjoint.at[0, 0], state, local_sem.at[1])
    snap_copy = pltpu.make_async_copy(snapshots.at[0, 0], snaps, local_sem.at[2])
    resid_copy = pltpu.make_async_copy(residuals, resid, local_sem.at[3])
    recs_copy = pltpu.make_async_copy(receivers, recs, local_sem.at[4])
    offset_copy = pltpu.make_async_copy(offsets, offset, local_sem.at[5])
    source_copy = pltpu.make_async_copy(sources, source_at, local_sem.at[6])
    for copy in (recs_copy, resid_copy, snap_copy, own_copy, state_copy, offset_copy, source_copy):
        copy.start()
    pl.semaphore_wait(barrier, tiles - 1)

    def push(src, dst, send, recv, to):
        return pltpu.make_async_remote_copy(
            src_ref=src,
            dst_ref=dst,
            send_sem=send,
            recv_sem=recv,
            device_id={"tile": to},
            device_id_type=MESH,
        )

    def when_in(t, fn):
        pl.when(jnp.logical_and(t >= 0, t < tiles))(fn)

    slot_x = 5 - 4 * xbit
    slot_z = 1 + 4 * xbit
    to_core = 2 * core - 1

    def send_x(f):
        return push(params.at[f], window.at[slot_z, f], p_send.at[0], p_recv.at[f], xn)

    send_own = push(params, window.at[2 + 2 * core], p_send.at[1], p_recv.at[10], partner)
    send_far = push(params, window.at[6 - 6 * core], p_send.at[2], p_recv.at[11], far)
    for f in range(nf):
        send_x(f).start()
    send_own.start()
    when_in(far, send_far.start)

    def on_z(f):
        block = window.at[slot_x, f]
        return push(block, window.at[slot_z, f], p_send.at[3], p_recv.at[5 + f], zf)

    def relay_x(f):
        block = window.at[slot_x, f]
        return push(block, window.at[slot_x + to_core, f], p_send.at[4], p_recv.at[12], partner)

    def relay_z(f):
        block = window.at[slot_z, f]
        return push(block, window.at[slot_z + to_core, f], p_send.at[5], p_recv.at[13], partner)

    def got(block, sem):
        push(block, block, p_send.at[0], sem, partner).wait_recv()

    def gone(block, sem):
        push(block, block, sem, p_recv.at[0], partner).wait_send()

    recs_copy.wait()
    resid_copy.wait()
    snap_copy.wait()
    cells = recs[...]
    lanes = cells.shape[1]
    rows = nx * ny
    blocks = [(r, c) for r in range(ny // 8) for c in range(nz // 128)]

    def pass_z(f):
        def go():
            got(window.at[slot_z, f], p_recv.at[5 + f])
            relay_z(f).start()

        when_in(zr, go)

    @pl.loop(0, STEPS)
    def _(s):
        @pl.when(s < nf)
        def _():
            got(window.at[slot_x, s], p_recv.at[s])
            when_in(zf, lambda: on_z(s).start())
            relay_x(s).start()

        @pl.when(s >= 2)
        def _():
            pass_z(s - 2)

        def velocity(i):
            planes = []
            for c in range(3):
                u = snaps[s, c, i].astype(jnp.float32)
                fields[s, 7 + c, i] = u
                planes.append(
                    [[u[r : r + 8, k : k + 128] for k in range(0, nz, 128)] for r in range(0, ny, 8)]
                )
            return planes

        def picker(plane):
            return lambda r, c: plane[r][c]

        before, here = None, velocity(0)
        for i in range(nx):
            after = velocity(i + 1) if i + 1 < nx else None
            strains = strains_of(
                here,
                None if before is None else picker(before[0]),
                None if after is None else [picker(after[1]), picker(after[2])],
            )
            for r, c in blocks:
                fxx, fyy, fzz, fxy, fxz, fyz = strains(r, c)
                trace = fxx + fyy + fzz
                for k, value in enumerate((fxx, fyy, fzz, 0.5 * fxy, fxz, fyz, trace)):
                    fields[(s, k, i, *block_of(r, c))] = value
            before, here = here, after

        row_hit = lax.broadcasted_iota(jnp.int32, (rows, lanes), 0) == lax.div(cells, nz)
        col_hit = lax.broadcasted_iota(jnp.int32, (nz, lanes), 0) == lax.rem(cells, nz)
        columns = jnp.where(col_hit, 1.0, 0.0).astype(jnp.bfloat16)
        rest = resid[s]
        left = []
        for part in range(3):
            piece = rest.astype(jnp.bfloat16).astype(jnp.float32)
            rest = rest - piece
            left.append(jnp.where(row_hit, piece, 0.0).astype(jnp.bfloat16))
        terms = lax.dot_general(
            jnp.concatenate(left, axis=0),
            columns,
            (((1,), (1,)), ((), ())),
            preferred_element_type=jnp.float32,
        )
        total = terms[:rows] + (terms[rows : 2 * rows] + terms[2 * rows :])
        inject[s] = total.reshape(nx, ny, nz)

    pass_z(nf - 1)
    got(window.at[4 - 2 * core], p_recv.at[10])
    when_in(far, lambda: got(window.at[6 * core], p_recv.at[11]))
    got(window.at[slot_x - to_core], p_recv.at[12])
    when_in(zr, lambda: got(window.at[slot_z - to_core], p_recv.at[13]))
    own_copy.wait()
    state_copy.wait()

    offset_copy.wait()
    source_copy.wait()
    rel = jnp.clip(offset[0] - me + REACH, 0, REACH)
    for j in range(APER):
        b, c11, c13, c33, c44 = [window[rel + j, f] for f in range(5)]
        here = slice(j * slab, (j + 1) * slab)
        coef[0, here] = STEP_H * b
        coef[1, here] = STEP_H * c13
        coef[2, here] = STEP_H * (c11 - c13)
        coef[3, here] = STEP_H * (c33 - c13)
        coef[4, here] = STEP_H * c44
        coef[5, here] = (0.5 * STEP_H) * (c11 - c13)

    grad[...] = jnp.zeros_like(grad)

    @pl.loop(0, STEPS)
    def _(s):
        def velocity(i):
            sxy, sxz, syy, syz, szz = [read(state, k, i) for k in (6, 7, 4, 8, 5)]
            sxy_y, sxz_z = shifted(sxy, 0, -1), shifted(sxz, 1, -1)
            syy_y, syz_z = shifted(syy, 0, 1), shifted(syz, 1, -1)
            syz_y, szz_z = shifted(syz, 0, -1), shifted(szz, 1, 1)
            for r, c in blocks:
                at = block_of(r, c)
                hb = coef[(0, i, *at)]
                sxx = state[(3, i, *at)]
                xy, xz, yy, yz, zz = [f[r][c] for f in (sxy, sxz, syy, syz, szz)]
                dxx = state[(3, i + 1, *at)] - sxx if i + 1 < nx else -sxx
                dxy = xy - state[(6, i - 1, *at)] if i > 0 else xy
                dxz = xz - state[(7, i - 1, *at)] if i > 0 else xz
                ax = dxx + ((xy - sxy_y(r, c)) + (xz - sxz_z(r, c)))
                ay = dxy + ((syy_y(r, c) - yy) + (yz - syz_z(r, c)))
                az = dxz + ((yz - syz_y(r, c)) + (szz_z(r, c) - zz))
                state[(0, i, *at)] += hb * ax
                state[(1, i, *at)] += hb * ay
                state[(2, i, *at)] = (state[(2, i, *at)] + inject[(s, i, *at)]) + hb * az

        def stress(i):
            here = [read(state, k, i) for k in range(3)]

            def picker(k, plane):
                return lambda r, c: state[(k, plane, *block_of(r, c))]

            strains = strains_of(
                here,
                picker(0, i - 1) if i > 0 else None,
                [picker(1, i + 1), picker(2, i + 1)] if i + 1 < nx else None,
            )
            for r, c in blocks:
                at = block_of(r, c)
                vx, vy, vz = [v[r][c] for v in here]
                exx, eyy, ezz, exy, exz, eyz = strains(r, c)
                h13, d11, d33, h44, h66 = [coef[(k, i, *at)] for k in range(1, 6)]
                trace = exx + eyy + ezz
                common = h13 * trace
                state[(3, i, *at)] += common + d11 * exx
                state[(4, i, *at)] += common + d11 * eyy
                state[(5, i, *at)] += common + d33 * ezz
                state[(6, i, *at)] += h66 * exy
                state[(7, i, *at)] += h44 * exz
                state[(8, i, *at)] += h44 * eyz
                fxx, fyy, fzz, fxy, fxz, fyz, ftrace, ux, uy, uz = [
                    fields[(s, k, i, *at)] for k in range(10)
                ]
                grad[(0, i, *at)] += vx * ux + vy * uy + vz * uz
                grad[(1, i, *at)] += exx * fxx + eyy * fyy + exy * fxy
                grad[(2, i, *at)] += trace * ftrace
                grad[(3, i, *at)] += ezz * fzz
                grad[(4, i, *at)] += exz * fxz + eyz * fyz

        velocity(0)
        for i in range(nx):
            if i + 1 < nx:
                velocity(i + 1)
            stress(i)

    source = source_at[0, 0]
    sx = lax.div(source, ny * nz)
    sy = lax.rem(lax.div(source, nz), ny)
    sz = lax.rem(source, nz)
    dy = lax.broadcasted_iota(jnp.int32, (ny, nz), 0) - sy
    dz = lax.broadcasted_iota(jnp.int32, (ny, nz), 1) - sz
    flat = dy * dy + dz * dz
    for i in range(nx):
        dx = i - sx
        d2 = (flat + dx * dx).astype(jnp.float32)
        weight = d2 / (d2 + float(MUTE * MUTE))
        k11, k33 = grad[1, i], grad[3, i]
        grad[2, i] = (grad[2, i] - k11 - k33) * weight
        grad[1, i] = k11 * weight
        grad[3, i] = k33 * weight
        grad[0, i] = grad[0, i] * weight
        grad[4, i] = grad[4, i] * weight

    def place(pos):
        j = pos - rel
        ok = jnp.logical_and(j >= 0, j < APER)
        start = slab * jnp.clip(j, 0, APER - 1)
        for f in range(5):
            for k in range(slab):
                gwin[pos, f, k] = jnp.where(ok, grad[f, start + k], 0.0)

    pair = [
        push(gwin.at[pos - to_core], fromp.at[k], g_send.at[k], g_recv.at[10 + k], partner)
        for k, pos in enumerate((slot_z, slot_x, REACH))
    ]
    to_far = push(gwin.at[6 * core], landed.at[2], g_send.at[5], g_recv.at[13], far)
    for k, pos in enumerate((slot_z, slot_x, REACH)):
        place(pos - to_core)
        pair[k].start()
    place(slot_z)
    place(6 * core)
    place(slot_x)
    place(REACH)

    def to_z(f):
        return push(sumbuf.at[0, f], landed.at[0, f], g_send.at[3], g_recv.at[5 + f], zr)

    def to_x(f):
        return push(sumbuf.at[1, f], landed.at[1, f], g_send.at[4], g_recv.at[f], xn)

    pair[0].wait_recv()
    for f in range(nf):
        sumbuf[0, f] = gwin[slot_z, f] + fromp[0, f]
        when_in(zr, to_z(f).start)
    when_in(far, to_far.start)
    pair[1].wait_recv()
    for f in range(nf):
        sumbuf[1, f] = gwin[slot_x, f] + fromp[1, f]

        def join(f=f):
            got(landed.at[0, f], g_recv.at[5 + f])
            sumbuf[1, f] += landed[0, f]

        when_in(zf, join)
        to_x(f).start()
    pair[2].wait_recv()
    out[...] = gwin[REACH] + fromp[2]

    def join_far():
        got(landed.at[2], g_recv.at[13])
        out[...] += landed[2]

    when_in(far, join_far)

    lane = lax.broadcasted_iota(jnp.int32, (1, 128), 1)
    row = jnp.zeros((1, 128), jnp.float32)
    for f in range(nf):
        got(landed.at[1, f], g_recv.at[f])
        total = out[f] + landed[1, f]
        out[f] = total
        biggest = jnp.max(jnp.abs(total), axis=(0, 1, 2), keepdims=True)[0]
        row = jnp.where(lane == f, biggest, row)
    mine[...] = row

    def max_copy(d):
        to = lax.rem(me + d, tiles)
        return push(mine, maxima.at[d - 1], m_send.at[0], m_recv.at[0], to)

    @pl.loop(1, tiles)
    def _(d):
        max_copy(d).start()

    store = pltpu.make_async_copy(out, summed, local_sem.at[7])
    store.start()

    gone(params, p_send.at[0])
    send_own.wait_send()
    when_in(far, send_far.wait_send)
    when_in(zf, lambda: gone(window.at[slot_x], p_send.at[3]))
    gone(window.at[slot_x], p_send.at[4])
    when_in(zr, lambda: gone(window.at[slot_z], p_send.at[5]))
    for copy in pair:
        copy.wait_send()
    when_in(far, to_far.wait_send)
    when_in(zr, lambda: gone(sumbuf.at[0], g_send.at[3]))
    gone(sumbuf.at[1], g_send.at[4])

    got(maxima, m_recv.at[0])
    scale = 1.0 / (jnp.maximum(jnp.max(maxima[...], axis=0), row) + EPSILON)
    for f in range(nf):
        factor = jnp.sum(jnp.where(lane == f, scale, 0.0), axis=1, keepdims=True)
        scales[f] = jnp.broadcast_to(factor, (1, nz))
    gone(maxima, m_send.at[0])
    store.wait()


def on_device(params, adjoint_state, snapshots, residuals, receivers, sources, offsets):
    tiles = lax.axis_size("tile")
    grid = adjoint_state.shape[3:]
    slab_shape = params.shape
    f32 = jnp.float32
    hbm = pl.BlockSpec(memory_space=pltpu.HBM)
    vmem = pl.BlockSpec(memory_space=pltpu.VMEM)
    dma = pltpu.SemaphoreType.DMA
    rows = jnp.transpose(residuals[0], (1, 0, 2))
    summed, scales = pl.pallas_call(
        functools.partial(kernel, tiles),
        out_shape=[
            jax.ShapeDtypeStruct(slab_shape, f32),
            jax.ShapeDtypeStruct((slab_shape[0], 1, slab_shape[3]), f32),
        ],
        in_specs=[hbm, hbm, hbm, hbm, hbm, hbm, hbm],
        out_specs=[hbm, vmem],
        scratch_shapes=[
            pltpu.VMEM(slab_shape, f32),
            pltpu.SMEM(offsets.shape, jnp.int32),
            pltpu.SMEM(sources.shape, jnp.int32),
            pltpu.VMEM((SPAN,) + slab_shape, f32),
            pltpu.VMEM((9,) + grid, f32),
            pltpu.VMEM((STEPS, 3) + grid, jnp.bfloat16),
            pltpu.VMEM(rows.shape, f32),
            pltpu.VMEM(receivers.shape[1:], jnp.int32),
            pltpu.VMEM((STEPS,) + grid, f32),
            pltpu.VMEM((STEPS, 10) + grid, f32),
            pltpu.VMEM((6,) + grid, f32),
            pltpu.VMEM((5,) + grid, f32),
            pltpu.VMEM((SPAN,) + slab_shape, f32),
            pltpu.VMEM((3,) + slab_shape, f32),
            pltpu.VMEM((2,) + slab_shape, f32),
            pltpu.VMEM((3,) + slab_shape, f32),
            pltpu.VMEM((1, 128), f32),
            pltpu.VMEM((tiles - 1, 1, 128), f32),
            dma((8,)),
            dma((6,)),
            dma((14,)),
            dma((6,)),
            dma((14,)),
            dma((1,)),
            dma((1,)),
        ],
        compiler_params=pltpu.CompilerParams(
            collective_id=0, has_side_effects=True, vmem_limit_bytes=56 * 1024 * 1024
        ),
    )(offsets, sources, params, adjoint_state, snapshots, rows, receivers[0])
    return summed * scales[:, :, None, :]


def solution(mesh):
    placed = (
        P("groups", "tile", None, None),
        P("tile", "groups", None, None, None, None),
        P("tile", "groups", None, None, None, None, None),
        P("tile", "groups", None, None),
        P("tile", "groups", None),
        P("tile", "groups"),
        P("tile"),
    )
    return jax.shard_map(
        on_device,
        mesh=mesh,
        in_specs=placed,
        out_specs=P("groups", "tile", None, None),
        check_vma=False,
    )
```

```python
import functools

import jax
import jax.numpy as jnp
from jax import lax
from jax.experimental import pallas as pl
from jax.experimental.pallas import tpu as pltpu
from jax.sharding import PartitionSpec as P

STEPS = 6
APER = 4
REACH = 3
MUTE = 4
SPAN = 2 * REACH + 1

STEP_H = 0.2
EPSILON = 1e-06
MESH = pl.DeviceIdType.MESH


def shifted(blocks, axis, by):
    rows, columns = len(blocks), len(blocks[0])
    size = blocks[0][0].shape[axis]
    place = lax.broadcasted_iota(jnp.int32, blocks[0][0].shape, axis)
    edge = place == (size - 1 if by == 1 else 0)
    turn = size - 1 if by == 1 else 1
    rolled = [[pltpu.roll(b, turn, axis) for b in row] for row in blocks]

    def at(r, c):
        nr, nc = (r + by, c) if axis == 0 else (r, c + by)
        beyond = rolled[nr][nc] if 0 <= nr < rows and 0 <= nc < columns else 0.0
        return jnp.where(edge, beyond, rolled[r][c])

    return at


def block_of(r, c):
    return pl.ds(8 * r, 8), pl.ds(128 * c, 128)


def read(ref, *at):
    ny, nz = ref.shape[-2:]
    return [[ref[(*at, *block_of(r, c))] for c in range(nz // 128)] for r in range(ny // 8)]


def strains_of(here, before, after):
    vx, vy, vz = here
    vx_y, vx_z = shifted(vx, 0, 1), shifted(vx, 1, 1)
    vy_y, vy_z = shifted(vy, 0, -1), shifted(vy, 1, 1)
    vz_y, vz_z = shifted(vz, 0, 1), shifted(vz, 1, -1)

    def at(r, c):
        x, y, z = vx[r][c], vy[r][c], vz[r][c]
        exx = x if before is None else x - before(r, c)
        eyy = y - vy_y(r, c)
        ezz = z - vz_z(r, c)
        dy = -y if after is None else after[0](r, c) - y
        dz = -z if after is None else after[1](r, c) - z
        exy = (vx_y(r, c) - x) + dy
        exz = (vx_z(r, c) - x) + dz
        eyz = (vy_z(r, c) - y) + (vz_y(r, c) - z)
        return exx, eyy, ezz, exy, exz, eyz

    return at


def gather_kernel(tiles, params, window, p_send, p_recv, local_sem):
    me = lax.axis_index("tile")
    core = lax.rem(me, 2)
    xbit = lax.rem(lax.div(me, 2), 2)
    partner = me + 1 - 2 * core
    far = me + 3 * (2 * core - 1)
    xn = me + 2 - 4 * xbit
    zf = me + 4 - 8 * xbit
    zr = me - 4 + 8 * xbit
    nf = params.shape[0]
    own_copy = pltpu.make_async_copy(params, window.at[REACH], local_sem.at[0])
    own_copy.start()

    barrier = pltpu.get_barrier_semaphore()
    greeted = [partner, xn, zf, zr, far]
    for t in greeted:

        def greet(t=t):
            pl.semaphore_signal(barrier, inc=1, device_id={"tile": t}, device_id_type=MESH)

        pl.when(jnp.logical_and(t >= 0, t < tiles))(greet)
    peers = 0
    for t in greeted:
        peers = peers + jnp.where(jnp.logical_and(t >= 0, t < tiles), 1, 0)
    pl.semaphore_wait(barrier, peers)

    def push(src, dst, send, recv, to):
        return pltpu.make_async_remote_copy(
            src_ref=src,
            dst_ref=dst,
            send_sem=send,
            recv_sem=recv,
            device_id={"tile": to},
            device_id_type=MESH,
        )

    def when_in(t, fn):
        pl.when(jnp.logical_and(t >= 0, t < tiles))(fn)

    slot_x = 5 - 4 * xbit
    slot_z = 1 + 4 * xbit
    to_core = 2 * core - 1

    def send_x(f):
        return push(params.at[f], window.at[slot_z, f], p_send.at[0], p_recv.at[f], xn)

    send_own = push(params, window.at[2 + 2 * core], p_send.at[1], p_recv.at[10], partner)
    send_far = push(params, window.at[6 - 6 * core], p_send.at[2], p_recv.at[11], far)
    for f in range(nf):
        send_x(f).start()
    send_own.start()
    when_in(far, send_far.start)

    def on_z(f):
        block = window.at[slot_x, f]
        return push(block, window.at[slot_z, f], p_send.at[3], p_recv.at[5 + f], zf)

    def relay_x(f):
        block = window.at[slot_x, f]
        return push(block, window.at[slot_x + to_core, f], p_send.at[4], p_recv.at[12], partner)

    def relay_z(f):
        block = window.at[slot_z, f]
        return push(block, window.at[slot_z + to_core, f], p_send.at[5], p_recv.at[13], partner)

    def got(block, sem):
        push(block, block, p_send.at[0], sem, partner).wait_recv()

    def gone(block, sem):
        push(block, block, sem, p_recv.at[0], partner).wait_send()

    def pass_z(f):
        def go():
            got(window.at[slot_z, f], p_recv.at[5 + f])
            relay_z(f).start()

        when_in(zr, go)

    for f in range(nf):
        got(window.at[slot_x, f], p_recv.at[f])
        when_in(zf, on_z(f).start)
        relay_x(f).start()
        if f >= 2:
            pass_z(f - 2)
    pass_z(nf - 2)
    pass_z(nf - 1)
    got(window.at[4 - 2 * core], p_recv.at[10])
    when_in(far, lambda: got(window.at[6 * core], p_recv.at[11]))
    got(window.at[slot_x - to_core], p_recv.at[12])
    when_in(zr, lambda: got(window.at[slot_z - to_core], p_recv.at[13]))
    own_copy.wait()
    gone(params, p_send.at[0])
    send_own.wait_send()
    when_in(far, send_far.wait_send)
    when_in(zf, lambda: gone(window.at[slot_x], p_send.at[3]))
    gone(window.at[slot_x], p_send.at[4])
    when_in(zr, lambda: gone(window.at[slot_z], p_send.at[5]))


def compute_kernel(
    offsets,
    sources,
    window,
    adjoint,
    snaps,
    resid,
    recs,
    gwin,
    state,
    inject,
    fields,
    coef,
    grad,
):
    me = lax.axis_index("tile")
    nx = state.shape[1]
    nf, slab = window.shape[1:3]
    ny, nz = state.shape[2], state.shape[3]
    state[...] = adjoint[...]
    cells = recs[...]
    lanes = cells.shape[1]
    rows = nx * ny
    blocks = [(r, c) for r in range(ny // 8) for c in range(nz // 128)]

    @pl.loop(0, STEPS)
    def _(s):
        def velocity(i):
            planes = []
            for c in range(3):
                u = snaps[s, c, i].astype(jnp.float32)
                fields[s, 7 + c, i] = u
                planes.append(
                    [[u[r : r + 8, k : k + 128] for k in range(0, nz, 128)] for r in range(0, ny, 8)]
                )
            return planes

        def picker(plane):
            return lambda r, c: plane[r][c]

        before, here = None, velocity(0)
        for i in range(nx):
            after = velocity(i + 1) if i + 1 < nx else None
            strains = strains_of(
                here,
                None if before is None else picker(before[0]),
                None if after is None else [picker(after[1]), picker(after[2])],
            )
            for r, c in blocks:
                fxx, fyy, fzz, fxy, fxz, fyz = strains(r, c)
                trace = fxx + fyy + fzz
                for k, value in enumerate((fxx, fyy, fzz, 0.5 * fxy, fxz, fyz, trace)):
                    fields[(s, k, i, *block_of(r, c))] = value
            before, here = here, after

        row_hit = lax.broadcasted_iota(jnp.int32, (rows, lanes), 0) == lax.div(cells, nz)
        col_hit = lax.broadcasted_iota(jnp.int32, (nz, lanes), 0) == lax.rem(cells, nz)
        columns = jnp.where(col_hit, 1.0, 0.0).astype(jnp.bfloat16)
        rest = resid[s]
        left = []
        for part in range(3):
            piece = rest.astype(jnp.bfloat16).astype(jnp.float32)
            rest = rest - piece
            left.append(jnp.where(row_hit, piece, 0.0).astype(jnp.bfloat16))
        terms = lax.dot_general(
            jnp.concatenate(left, axis=0),
            columns,
            (((1,), (1,)), ((), ())),
            preferred_element_type=jnp.float32,
        )
        total = terms[:rows] + (terms[rows : 2 * rows] + terms[2 * rows :])
        inject[s] = total.reshape(nx, ny, nz)

    rel = jnp.clip(offsets[0] - me + REACH, 0, REACH)
    for j in range(APER):
        b, c11, c13, c33, c44 = [window[rel + j, f] for f in range(5)]
        here = slice(j * slab, (j + 1) * slab)
        coef[0, here] = STEP_H * b
        coef[1, here] = STEP_H * c13
        coef[2, here] = STEP_H * (c11 - c13)
        coef[3, here] = STEP_H * (c33 - c13)
        coef[4, here] = STEP_H * c44
        coef[5, here] = (0.5 * STEP_H) * (c11 - c13)

    grad[...] = jnp.zeros_like(grad)

    @pl.loop(0, STEPS)
    def _(s):
        def velocity(i):
            sxy, sxz, syy, syz, szz = [read(state, k, i) for k in (6, 7, 4, 8, 5)]
            sxy_y, sxz_z = shifted(sxy, 0, -1), shifted(sxz, 1, -1)
            syy_y, syz_z = shifted(syy, 0, 1), shifted(syz, 1, -1)
            syz_y, szz_z = shifted(syz, 0, -1), shifted(szz, 1, 1)
            for r, c in blocks:
                at = block_of(r, c)
                hb = coef[(0, i, *at)]
                sxx = state[(3, i, *at)]
                xy, xz, yy, yz, zz = [f[r][c] for f in (sxy, sxz, syy, syz, szz)]
                dxx = state[(3, i + 1, *at)] - sxx if i + 1 < nx else -sxx
                dxy = xy - state[(6, i - 1, *at)] if i > 0 else xy
                dxz = xz - state[(7, i - 1, *at)] if i > 0 else xz
                ax = dxx + ((xy - sxy_y(r, c)) + (xz - sxz_z(r, c)))
                ay = dxy + ((syy_y(r, c) - yy) + (yz - syz_z(r, c)))
                az = dxz + ((yz - syz_y(r, c)) + (szz_z(r, c) - zz))
                state[(0, i, *at)] += hb * ax
                state[(1, i, *at)] += hb * ay
                state[(2, i, *at)] = (state[(2, i, *at)] + inject[(s, i, *at)]) + hb * az

        def stress(i):
            here = [read(state, k, i) for k in range(3)]

            def picker(k, plane):
                return lambda r, c: state[(k, plane, *block_of(r, c))]

            strains = strains_of(
                here,
                picker(0, i - 1) if i > 0 else None,
                [picker(1, i + 1), picker(2, i + 1)] if i + 1 < nx else None,
            )
            for r, c in blocks:
                at = block_of(r, c)
                vx, vy, vz = [v[r][c] for v in here]
                exx, eyy, ezz, exy, exz, eyz = strains(r, c)
                h13, d11, d33, h44, h66 = [coef[(k, i, *at)] for k in range(1, 6)]
                trace = exx + eyy + ezz
                common = h13 * trace
                state[(3, i, *at)] += common + d11 * exx
                state[(4, i, *at)] += common + d11 * eyy
                state[(5, i, *at)] += common + d33 * ezz
                state[(6, i, *at)] += h66 * exy
                state[(7, i, *at)] += h44 * exz
                state[(8, i, *at)] += h44 * eyz
                fxx, fyy, fzz, fxy, fxz, fyz, ftrace, ux, uy, uz = [
                    fields[(s, k, i, *at)] for k in range(10)
                ]
                grad[(0, i, *at)] += vx * ux + vy * uy + vz * uz
                grad[(1, i, *at)] += exx * fxx + eyy * fyy + exy * fxy
                grad[(2, i, *at)] += trace * ftrace
                grad[(3, i, *at)] += ezz * fzz
                grad[(4, i, *at)] += exz * fxz + eyz * fyz

        velocity(0)
        for i in range(nx):
            if i + 1 < nx:
                velocity(i + 1)
            stress(i)

    source = sources[0, 0]
    sx = lax.div(source, ny * nz)
    sy = lax.rem(lax.div(source, nz), ny)
    sz = lax.rem(source, nz)
    dy = lax.broadcasted_iota(jnp.int32, (ny, nz), 0) - sy
    dz = lax.broadcasted_iota(jnp.int32, (ny, nz), 1) - sz
    flat = dy * dy + dz * dz
    for i in range(nx):
        dx = i - sx
        d2 = (flat + dx * dx).astype(jnp.float32)
        weight = d2 / (d2 + float(MUTE * MUTE))
        k11, k33 = grad[1, i], grad[3, i]
        grad[2, i] = (grad[2, i] - k11 - k33) * weight
        grad[1, i] = k11 * weight
        grad[3, i] = k33 * weight
        grad[0, i] = grad[0, i] * weight
        grad[4, i] = grad[4, i] * weight

    def place(pos):
        j = pos - rel
        ok = jnp.logical_and(j >= 0, j < APER)
        start = slab * jnp.clip(j, 0, APER - 1)
        for f in range(5):
            for k in range(slab):
                gwin[pos, f, k] = jnp.where(ok, grad[f, start + k], 0.0)

    for pos in range(SPAN):
        place(pos)


def reduce_kernel(
    tiles, gwin, out, fromp, sumbuf, landed, mine, maxima, g_send, g_recv, m_send, m_recv
):
    me = lax.axis_index("tile")
    core = lax.rem(me, 2)
    xbit = lax.rem(lax.div(me, 2), 2)
    partner = me + 1 - 2 * core
    far = me + 3 * (2 * core - 1)
    xn = me + 2 - 4 * xbit
    zf = me + 4 - 8 * xbit
    zr = me - 4 + 8 * xbit
    nf = gwin.shape[1]

    barrier = pltpu.get_barrier_semaphore()

    @pl.loop(1, tiles)
    def _(d):
        pl.semaphore_signal(
            barrier, inc=1, device_id={"tile": lax.rem(me + d, tiles)}, device_id_type=MESH
        )

    pl.semaphore_wait(barrier, tiles - 1)

    def push(src, dst, send, recv, to):
        return pltpu.make_async_remote_copy(
            src_ref=src,
            dst_ref=dst,
            send_sem=send,
            recv_sem=recv,
            device_id={"tile": to},
            device_id_type=MESH,
        )

    def when_in(t, fn):
        pl.when(jnp.logical_and(t >= 0, t < tiles))(fn)

    slot_x = 5 - 4 * xbit
    slot_z = 1 + 4 * xbit
    to_core = 2 * core - 1

    def got(block, sem):
        push(block, block, g_send.at[0], sem, partner).wait_recv()

    def gone(block, sem):
        push(block, block, sem, g_recv.at[0], partner).wait_send()

    pair = [
        push(gwin.at[pos - to_core], fromp.at[k], g_send.at[k], g_recv.at[10 + k], partner)
        for k, pos in enumerate((slot_z, slot_x, REACH))
    ]
    to_far = push(gwin.at[6 * core], landed.at[2], g_send.at[5], g_recv.at[13], far)
    for k, pos in enumerate((slot_z, slot_x, REACH)):
        pair[k].start()

    def to_z(f):
        return push(sumbuf.at[0, f], landed.at[0, f], g_send.at[3], g_recv.at[5 + f], zr)

    def to_x(f):
        return push(sumbuf.at[1, f], landed.at[1, f], g_send.at[4], g_recv.at[f], xn)

    pair[0].wait_recv()
    for f in range(nf):
        sumbuf[0, f] = gwin[slot_z, f] + fromp[0, f]
        when_in(zr, to_z(f).start)
    when_in(far, to_far.start)
    pair[1].wait_recv()
    for f in range(nf):
        sumbuf[1, f] = gwin[slot_x, f] + fromp[1, f]

        def join(f=f):
            got(landed.at[0, f], g_recv.at[5 + f])
            sumbuf[1, f] += landed[0, f]

        when_in(zf, join)
        to_x(f).start()
    pair[2].wait_recv()
    out[...] = gwin[REACH] + fromp[2]

    def join_far():
        got(landed.at[2], g_recv.at[13])
        out[...] += landed[2]

    when_in(far, join_far)

    lane = lax.broadcasted_iota(jnp.int32, (1, 128), 1)
    row = jnp.zeros((1, 128), jnp.float32)
    for f in range(nf):
        got(landed.at[1, f], g_recv.at[f])
        total = out[f] + landed[1, f]
        out[f] = total
        biggest = jnp.max(jnp.abs(total), axis=(0, 1, 2), keepdims=True)[0]
        row = jnp.where(lane == f, biggest, row)
    mine[...] = row

    def max_copy(d):
        to = lax.rem(me + d, tiles)
        return push(mine, maxima.at[d - 1], m_send.at[0], m_recv.at[0], to)

    @pl.loop(1, tiles)
    def _(d):
        max_copy(d).start()

    for copy in pair:
        copy.wait_send()
    when_in(far, to_far.wait_send)
    when_in(zr, lambda: gone(sumbuf.at[0], g_send.at[3]))
    gone(sumbuf.at[1], g_send.at[4])
    got(maxima, m_recv.at[0])
    scale = 1.0 / (jnp.maximum(jnp.max(maxima[...], axis=0), row) + EPSILON)
    for f in range(nf):
        out[f] = out[f] * jnp.sum(jnp.where(lane == f, scale, 0.0), axis=1, keepdims=True)
    gone(maxima, m_send.at[0])


def on_device(params, adjoint_state, snapshots, residuals, receivers, sources, offsets):
    tiles = lax.axis_size("tile")
    grid = adjoint_state.shape[3:]
    slab_shape = params.shape
    f32 = jnp.float32
    hbm = pl.BlockSpec(memory_space=pl.ANY)
    smem = pl.BlockSpec(memory_space=pltpu.SMEM)
    vmem = pl.BlockSpec(memory_space=pltpu.VMEM)
    dma = pltpu.SemaphoreType.DMA
    mib = 1024 * 1024
    rows = jnp.transpose(residuals[0], (1, 0, 2))
    window = pl.pallas_call(
        functools.partial(gather_kernel, tiles),
        out_shape=jax.ShapeDtypeStruct((SPAN,) + slab_shape, f32),
        in_specs=[hbm],
        out_specs=vmem,
        scratch_shapes=[dma((6,)), dma((14,)), dma((1,))],
        compiler_params=pltpu.CompilerParams(
            collective_id=0, has_side_effects=True, vmem_limit_bytes=16 * mib
        ),
    )(params)
    gwin = pl.pallas_call(
        compute_kernel,
        out_shape=jax.ShapeDtypeStruct((SPAN,) + slab_shape, f32),
        in_specs=[smem, smem, vmem, vmem, vmem, vmem, vmem],
        out_specs=vmem,
        scratch_shapes=[
            pltpu.VMEM((9,) + grid, f32),
            pltpu.VMEM((STEPS,) + grid, f32),
            pltpu.VMEM((STEPS, 10) + grid, f32),
            pltpu.VMEM((6,) + grid, f32),
            pltpu.VMEM((5,) + grid, f32),
        ],
        compiler_params=pltpu.CompilerParams(vmem_limit_bytes=32 * mib),
    )(offsets, sources, window, adjoint_state[0, 0], snapshots[0, 0], rows, receivers[0])
    return pl.pallas_call(
        functools.partial(reduce_kernel, tiles),
        out_shape=jax.ShapeDtypeStruct(slab_shape, f32),
        in_specs=[vmem],
        out_specs=vmem,
        scratch_shapes=[
            pltpu.VMEM((3,) + slab_shape, f32),
            pltpu.VMEM((2,) + slab_shape, f32),
            pltpu.VMEM((3,) + slab_shape, f32),
            pltpu.VMEM((1, 128), f32),
            pltpu.VMEM((tiles - 1, 1, 128), f32),
            dma((6,)),
            dma((14,)),
            dma((1,)),
            dma((1,)),
        ],
        compiler_params=pltpu.CompilerParams(
            collective_id=1, has_side_effects=True, vmem_limit_bytes=16 * mib
        ),
    )(gwin)


def solution(mesh):
    placed = (
        P("groups", "tile", None, None),
        P("tile", "groups", None, None, None, None),
        P("tile", "groups", None, None, None, None, None),
        P("tile", "groups", None, None),
        P("tile", "groups", None),
        P("tile", "groups"),
        P("tile"),
    )
    return jax.shard_map(
        on_device,
        mesh=mesh,
        in_specs=placed,
        out_specs=P("groups", "tile", None, None),
        check_vma=False,
    )
```

```python
import functools

import jax
import jax.numpy as jnp
from jax import lax
from jax.experimental import pallas as pl
from jax.experimental.pallas import tpu as pltpu
from jax.sharding import PartitionSpec as P

STEPS = 6
APER = 4
REACH = 3
MUTE = 4
SPAN = 2 * REACH + 1

STEP_H = 0.2
EPSILON = 1e-06
MESH = pl.DeviceIdType.MESH


def shifted(blocks, axis, by):
    rows, columns = len(blocks), len(blocks[0])
    size = blocks[0][0].shape[axis]
    place = lax.broadcasted_iota(jnp.int32, blocks[0][0].shape, axis)
    edge = place == (size - 1 if by == 1 else 0)
    turn = size - 1 if by == 1 else 1
    rolled = [[pltpu.roll(b, turn, axis) for b in row] for row in blocks]

    def at(r, c):
        nr, nc = (r + by, c) if axis == 0 else (r, c + by)
        beyond = rolled[nr][nc] if 0 <= nr < rows and 0 <= nc < columns else 0.0
        return jnp.where(edge, beyond, rolled[r][c])

    return at


def block_of(r, c):
    return pl.ds(8 * r, 8), pl.ds(128 * c, 128)


def read(ref, *at):
    ny, nz = ref.shape[-2:]
    return [[ref[(*at, *block_of(r, c))] for c in range(nz // 128)] for r in range(ny // 8)]


def strains_of(here, before, after):
    vx, vy, vz = here
    vx_y, vx_z = shifted(vx, 0, 1), shifted(vx, 1, 1)
    vy_y, vy_z = shifted(vy, 0, -1), shifted(vy, 1, 1)
    vz_y, vz_z = shifted(vz, 0, 1), shifted(vz, 1, -1)

    def at(r, c):
        x, y, z = vx[r][c], vy[r][c], vz[r][c]
        exx = x if before is None else x - before(r, c)
        eyy = y - vy_y(r, c)
        ezz = z - vz_z(r, c)
        dy = -y if after is None else after[0](r, c) - y
        dz = -z if after is None else after[1](r, c) - z
        exy = (vx_y(r, c) - x) + dy
        exz = (vx_z(r, c) - x) + dz
        eyz = (vy_z(r, c) - y) + (vz_y(r, c) - z)
        return exx, eyy, ezz, exy, exz, eyz

    return at


def kernel(
    tiles,
    offsets,
    sources,
    params,
    adjoint,
    snapshots,
    residuals,
    receivers,
    out,
    offset,
    source_at,
    window,
    state,
    snaps,
    resid,
    recs,
    inject,
    fields,
    coef,
    grad,
    gwin,
    fromp,
    sumbuf,
    landed,
    mine,
    maxima,
    local_sem,
    p_send,
    p_recv,
    g_send,
    g_recv,
    m_send,
    m_recv,
):
    me = lax.axis_index("tile")
    core = lax.rem(me, 2)
    xbit = lax.rem(lax.div(me, 2), 2)
    partner = me + 1 - 2 * core
    far = me + 3 * (2 * core - 1)
    xn = me + 2 - 4 * xbit
    zf = me + 4 - 8 * xbit
    zr = me - 4 + 8 * xbit
    nx = state.shape[1]
    nf, slab = params.shape[:2]
    ny, nz = state.shape[2], state.shape[3]

    barrier = pltpu.get_barrier_semaphore()

    @pl.loop(1, tiles)
    def _(d):
        pl.semaphore_signal(
            barrier, inc=1, device_id={"tile": lax.rem(me + d, tiles)}, device_id_type=MESH
        )

    own_copy = pltpu.make_async_copy(params, window.at[REACH], local_sem.at[0])
    state_copy = pltpu.make_async_copy(adjoint.at[0, 0], state, local_sem.at[1])
    snap_copy = pltpu.make_async_copy(snapshots.at[0, 0], snaps, local_sem.at[2])
    resid_copy = pltpu.make_async_copy(residuals, resid, local_sem.at[3])
    recs_copy = pltpu.make_async_copy(receivers, recs, local_sem.at[4])
    offset_copy = pltpu.make_async_copy(offsets, offset, local_sem.at[5])
    source_copy = pltpu.make_async_copy(sources, source_at, local_sem.at[6])
    for copy in (recs_copy, resid_copy, snap_copy, own_copy, state_copy, offset_copy, source_copy):
        copy.start()
    pl.semaphore_wait(barrier, tiles - 1)

    def push(src, dst, send, recv, to):
        return pltpu.make_async_remote_copy(
            src_ref=src,
            dst_ref=dst,
            send_sem=send,
            recv_sem=recv,
            device_id={"tile": to},
            device_id_type=MESH,
        )

    def when_in(t, fn):
        pl.when(jnp.logical_and(t >= 0, t < tiles))(fn)

    slot_x = 5 - 4 * xbit
    slot_z = 1 + 4 * xbit
    to_core = 2 * core - 1

    def send_x(f):
        return push(params.at[f], window.at[slot_z, f], p_send.at[0], p_recv.at[f], xn)

    send_own = push(params, window.at[2 + 2 * core], p_send.at[1], p_recv.at[10], partner)
    send_far = push(params, window.at[6 - 6 * core], p_send.at[2], p_recv.at[11], far)
    for f in range(nf):
        send_x(f).start()
    send_own.start()
    when_in(far, send_far.start)

    def on_z(f):
        block = window.at[slot_x, f]
        return push(block, window.at[slot_z, f], p_send.at[3], p_recv.at[5 + f], zf)

    def relay_x(f):
        block = window.at[slot_x, f]
        return push(block, window.at[slot_x + to_core, f], p_send.at[4], p_recv.at[12], partner)

    def relay_z(f):
        block = window.at[slot_z, f]
        return push(block, window.at[slot_z + to_core, f], p_send.at[5], p_recv.at[13], partner)

    def got(block, sem):
        push(block, block, p_send.at[0], sem, partner).wait_recv()

    def gone(block, sem):
        push(block, block, sem, p_recv.at[0], partner).wait_send()

    recs_copy.wait()
    resid_copy.wait()
    snap_copy.wait()
    cells = recs[...]
    lanes = cells.shape[1]
    rows = nx * ny
    blocks = [(r, c) for r in range(ny // 8) for c in range(nz // 128)]

    def pass_z(f):
        def go():
            got(window.at[slot_z, f], p_recv.at[5 + f])
            relay_z(f).start()

        when_in(zr, go)

    @pl.loop(0, STEPS)
    def _(s):
        @pl.when(s < nf)
        def _():
            got(window.at[slot_x, s], p_recv.at[s])
            when_in(zf, lambda: on_z(s).start())
            relay_x(s).start()

        @pl.when(s >= 2)
        def _():
            pass_z(s - 2)

        def velocity(i):
            planes = []
            for c in range(3):
                u = snaps[s, c, i].astype(jnp.float32)
                fields[s, 7 + c, i] = u
                planes.append(
                    [[u[r : r + 8, k : k + 128] for k in range(0, nz, 128)] for r in range(0, ny, 8)]
                )
            return planes

        def picker(plane):
            return lambda r, c: plane[r][c]

        before, here = None, velocity(0)
        for i in range(nx):
            after = velocity(i + 1) if i + 1 < nx else None
            strains = strains_of(
                here,
                None if before is None else picker(before[0]),
                None if after is None else [picker(after[1]), picker(after[2])],
            )
            for r, c in blocks:
                fxx, fyy, fzz, fxy, fxz, fyz = strains(r, c)
                trace = fxx + fyy + fzz
                for k, value in enumerate((fxx, fyy, fzz, 0.5 * fxy, fxz, fyz, trace)):
                    fields[(s, k, i, *block_of(r, c))] = value
            before, here = here, after

        row_hit = lax.broadcasted_iota(jnp.int32, (rows, lanes), 0) == lax.div(cells, nz)
        col_hit = lax.broadcasted_iota(jnp.int32, (nz, lanes), 0) == lax.rem(cells, nz)
        columns = jnp.where(col_hit, 1.0, 0.0).astype(jnp.bfloat16)
        rest = resid[s]
        left = []
        for part in range(3):
            piece = rest.astype(jnp.bfloat16).astype(jnp.float32)
            rest = rest - piece
            left.append(jnp.where(row_hit, piece, 0.0).astype(jnp.bfloat16))
        terms = lax.dot_general(
            jnp.concatenate(left, axis=0),
            columns,
            (((1,), (1,)), ((), ())),
            preferred_element_type=jnp.float32,
        )
        total = terms[:rows] + (terms[rows : 2 * rows] + terms[2 * rows :])
        inject[s] = total.reshape(nx, ny, nz)

    pass_z(nf - 1)
    got(window.at[4 - 2 * core], p_recv.at[10])
    when_in(far, lambda: got(window.at[6 * core], p_recv.at[11]))
    got(window.at[slot_x - to_core], p_recv.at[12])
    when_in(zr, lambda: got(window.at[slot_z - to_core], p_recv.at[13]))
    own_copy.wait()
    state_copy.wait()

    offset_copy.wait()
    source_copy.wait()
    rel = jnp.clip(offset[0] - me + REACH, 0, REACH)
    for j in range(APER):
        b, c11, c13, c33, c44 = [window[rel + j, f] for f in range(5)]
        here = slice(j * slab, (j + 1) * slab)
        coef[0, here] = STEP_H * b
        coef[1, here] = STEP_H * c13
        coef[2, here] = STEP_H * (c11 - c13)
        coef[3, here] = STEP_H * (c33 - c13)
        coef[4, here] = STEP_H * c44
        coef[5, here] = (0.5 * STEP_H) * (c11 - c13)

    grad[...] = jnp.zeros_like(grad)

    @pl.loop(0, STEPS)
    def _(s):
        def velocity(i):
            sxy, sxz, syy, syz, szz = [read(state, k, i) for k in (6, 7, 4, 8, 5)]
            sxy_y, sxz_z = shifted(sxy, 0, -1), shifted(sxz, 1, -1)
            syy_y, syz_z = shifted(syy, 0, 1), shifted(syz, 1, -1)
            syz_y, szz_z = shifted(syz, 0, -1), shifted(szz, 1, 1)
            for r, c in blocks:
                at = block_of(r, c)
                hb = coef[(0, i, *at)]
                sxx = state[(3, i, *at)]
                xy, xz, yy, yz, zz = [f[r][c] for f in (sxy, sxz, syy, syz, szz)]
                dxx = state[(3, i + 1, *at)] - sxx if i + 1 < nx else -sxx
                dxy = xy - state[(6, i - 1, *at)] if i > 0 else xy
                dxz = xz - state[(7, i - 1, *at)] if i > 0 else xz
                ax = dxx + ((xy - sxy_y(r, c)) + (xz - sxz_z(r, c)))
                ay = dxy + ((syy_y(r, c) - yy) + (yz - syz_z(r, c)))
                az = dxz + ((yz - syz_y(r, c)) + (szz_z(r, c) - zz))
                state[(0, i, *at)] += hb * ax
                state[(1, i, *at)] += hb * ay
                state[(2, i, *at)] = (state[(2, i, *at)] + inject[(s, i, *at)]) + hb * az

        def stress(i):
            here = [read(state, k, i) for k in range(3)]

            def picker(k, plane):
                return lambda r, c: state[(k, plane, *block_of(r, c))]

            strains = strains_of(
                here,
                picker(0, i - 1) if i > 0 else None,
                [picker(1, i + 1), picker(2, i + 1)] if i + 1 < nx else None,
            )
            for r, c in blocks:
                at = block_of(r, c)
                vx, vy, vz = [v[r][c] for v in here]
                exx, eyy, ezz, exy, exz, eyz = strains(r, c)
                h13, d11, d33, h44, h66 = [coef[(k, i, *at)] for k in range(1, 6)]
                trace = exx + eyy + ezz
                common = h13 * trace
                state[(3, i, *at)] += common + d11 * exx
                state[(4, i, *at)] += common + d11 * eyy
                state[(5, i, *at)] += common + d33 * ezz
                state[(6, i, *at)] += h66 * exy
                state[(7, i, *at)] += h44 * exz
                state[(8, i, *at)] += h44 * eyz
                fxx, fyy, fzz, fxy, fxz, fyz, ftrace, ux, uy, uz = [
                    fields[(s, k, i, *at)] for k in range(10)
                ]
                grad[(0, i, *at)] += vx * ux + vy * uy + vz * uz
                grad[(1, i, *at)] += exx * fxx + eyy * fyy + exy * fxy
                grad[(2, i, *at)] += trace * ftrace
                grad[(3, i, *at)] += ezz * fzz
                grad[(4, i, *at)] += exz * fxz + eyz * fyz

        velocity(0)
        for i in range(nx):
            if i + 1 < nx:
                velocity(i + 1)
            stress(i)

    source = source_at[0, 0]
    sx = lax.div(source, ny * nz)
    sy = lax.rem(lax.div(source, nz), ny)
    sz = lax.rem(source, nz)
    dy = lax.broadcasted_iota(jnp.int32, (ny, nz), 0) - sy
    dz = lax.broadcasted_iota(jnp.int32, (ny, nz), 1) - sz
    flat = dy * dy + dz * dz
    for i in range(nx):
        dx = i - sx
        d2 = (flat + dx * dx).astype(jnp.float32)
        weight = d2 / (d2 + float(MUTE * MUTE))
        k11, k33 = grad[1, i], grad[3, i]
        grad[2, i] = (grad[2, i] - k11 - k33) * weight
        grad[1, i] = k11 * weight
        grad[3, i] = k33 * weight
        grad[0, i] = grad[0, i] * weight
        grad[4, i] = grad[4, i] * weight

    def place(pos):
        j = pos - rel
        ok = jnp.logical_and(j >= 0, j < APER)
        start = slab * jnp.clip(j, 0, APER - 1)
        for f in range(5):
            for k in range(slab):
                gwin[pos, f, k] = jnp.where(ok, grad[f, start + k], 0.0)

    def pair_z(f):
        block = gwin.at[slot_z - to_core, f]
        return push(block, fromp.at[0, f], g_send.at[0], g_recv.at[10 + f], partner)

    def pair_x(f):
        block = gwin.at[slot_x - to_core, f]
        return push(block, fromp.at[1, f], g_send.at[1], g_recv.at[15 + f], partner)

    pair_own = push(gwin.at[REACH - to_core], fromp.at[2], g_send.at[2], g_recv.at[20], partner)

    def to_far(f):
        return push(gwin.at[6 * core, f], landed.at[2, f], g_send.at[5], g_recv.at[21], far)

    def to_z(f):
        return push(sumbuf.at[0, f], landed.at[0, f], g_send.at[3], g_recv.at[5 + f], zr)

    def to_x(f):
        return push(sumbuf.at[1, f], landed.at[1, f], g_send.at[4], g_recv.at[f], xn)

    place(slot_z - to_core)
    for f in range(nf):
        pair_z(f).start()
    place(6 * core)
    when_in(far, to_far(0).start)
    place(slot_x - to_core)
    for f in range(nf):
        pair_x(f).start()
    place(slot_z)
    for f in range(nf):
        pair_z(f).wait_recv()
        sumbuf[0, f] = gwin[slot_z, f] + fromp[0, f]
        when_in(zr, to_z(f).start)
    for f in range(1, nf):
        when_in(far, to_far(f).start)
    place(REACH - to_core)
    pair_own.start()
    place(slot_x)
    place(REACH)
    for f in range(nf):
        pair_x(f).wait_recv()
        sumbuf[1, f] = gwin[slot_x, f] + fromp[1, f]

        def join(f=f):
            got(landed.at[0, f], g_recv.at[5 + f])
            sumbuf[1, f] += landed[0, f]

        when_in(zf, join)
        to_x(f).start()
    pair_own.wait_recv()
    out[...] = gwin[REACH] + fromp[2]

    def join_far():
        got(landed.at[2], g_recv.at[21])
        out[...] += landed[2]

    when_in(far, join_far)

    lane = lax.broadcasted_iota(jnp.int32, (1, 128), 1)
    row = jnp.zeros((1, 128), jnp.float32)
    for f in range(nf):
        got(landed.at[1, f], g_recv.at[f])
        total = out[f] + landed[1, f]
        out[f] = total
        biggest = jnp.max(jnp.abs(total), axis=(0, 1, 2), keepdims=True)[0]
        row = jnp.where(lane == f, biggest, row)
    mine[...] = row

    def max_copy(d):
        to = lax.rem(me + d, tiles)
        return push(mine, maxima.at[d - 1], m_send.at[0], m_recv.at[0], to)

    @pl.loop(1, tiles)
    def _(d):
        max_copy(d).start()

    gone(params, p_send.at[0])
    send_own.wait_send()
    when_in(far, send_far.wait_send)
    when_in(zf, lambda: gone(window.at[slot_x], p_send.at[3]))
    gone(window.at[slot_x], p_send.at[4])
    when_in(zr, lambda: gone(window.at[slot_z], p_send.at[5]))
    gone(fromp.at[0], g_send.at[0])
    gone(fromp.at[1], g_send.at[1])
    pair_own.wait_send()
    when_in(far, lambda: gone(landed.at[2], g_send.at[5]))
    when_in(zr, lambda: gone(sumbuf.at[0], g_send.at[3]))
    gone(sumbuf.at[1], g_send.at[4])

    got(maxima, m_recv.at[0])
    scale = 1.0 / (jnp.maximum(jnp.max(maxima[...], axis=0), row) + EPSILON)
    for f in range(nf):
        out[f] = out[f] * jnp.sum(jnp.where(lane == f, scale, 0.0), axis=1, keepdims=True)
    gone(maxima, m_send.at[0])


def on_device(params, adjoint_state, snapshots, residuals, receivers, sources, offsets):
    tiles = lax.axis_size("tile")
    grid = adjoint_state.shape[3:]
    slab_shape = params.shape
    f32 = jnp.float32
    hbm = pl.BlockSpec(memory_space=pltpu.HBM)
    vmem = pl.BlockSpec(memory_space=pltpu.VMEM)
    dma = pltpu.SemaphoreType.DMA
    rows = jnp.transpose(residuals[0], (1, 0, 2))
    return pl.pallas_call(
        functools.partial(kernel, tiles),
        out_shape=jax.ShapeDtypeStruct(slab_shape, f32),
        in_specs=[hbm, hbm, hbm, hbm, hbm, hbm, hbm],
        out_specs=vmem,
        scratch_shapes=[
            pltpu.SMEM(offsets.shape, jnp.int32),
            pltpu.SMEM(sources.shape, jnp.int32),
            pltpu.VMEM((SPAN,) + slab_shape, f32),
            pltpu.VMEM((9,) + grid, f32),
            pltpu.VMEM((STEPS, 3) + grid, jnp.bfloat16),
            pltpu.VMEM(rows.shape, f32),
            pltpu.VMEM(receivers.shape[1:], jnp.int32),
            pltpu.VMEM((STEPS,) + grid, f32),
            pltpu.VMEM((STEPS, 10) + grid, f32),
            pltpu.VMEM((6,) + grid, f32),
            pltpu.VMEM((5,) + grid, f32),
            pltpu.VMEM((SPAN,) + slab_shape, f32),
            pltpu.VMEM((3,) + slab_shape, f32),
            pltpu.VMEM((2,) + slab_shape, f32),
            pltpu.VMEM((3,) + slab_shape, f32),
            pltpu.VMEM((1, 128), f32),
            pltpu.VMEM((tiles - 1, 1, 128), f32),
            dma((8,)),
            dma((6,)),
            dma((14,)),
            dma((6,)),
            dma((22,)),
            dma((1,)),
            dma((1,)),
        ],
        compiler_params=pltpu.CompilerParams(
            collective_id=0, has_side_effects=True, vmem_limit_bytes=56 * 1024 * 1024
        ),
    )(offsets, sources, params, adjoint_state, snapshots, rows, receivers[0])


def solution(mesh):
    placed = (
        P("groups", "tile", None, None),
        P("tile", "groups", None, None, None, None),
        P("tile", "groups", None, None, None, None, None),
        P("tile", "groups", None, None),
        P("tile", "groups", None),
        P("tile", "groups"),
        P("tile"),
    )
    return jax.shard_map(
        on_device,
        mesh=mesh,
        in_specs=placed,
        out_specs=P("groups", "tile", None, None),
        check_vma=False,
    )
```

```python
import functools

import jax
import jax.numpy as jnp
from jax import lax
from jax.experimental import pallas as pl
from jax.experimental.pallas import tpu as pltpu
from jax.sharding import PartitionSpec as P

STEPS = 6
APER = 4
REACH = 3
MUTE = 4
SPAN = 2 * REACH + 1

STEP_H = 0.2
EPSILON = 1e-06
MESH = pl.DeviceIdType.MESH


def shifted(blocks, axis, by):
    rows, columns = len(blocks), len(blocks[0])
    size = blocks[0][0].shape[axis]
    place = lax.broadcasted_iota(jnp.int32, blocks[0][0].shape, axis)
    edge = place == (size - 1 if by == 1 else 0)
    turn = size - 1 if by == 1 else 1
    rolled = [[pltpu.roll(b, turn, axis) for b in row] for row in blocks]

    def at(r, c):
        nr, nc = (r + by, c) if axis == 0 else (r, c + by)
        beyond = rolled[nr][nc] if 0 <= nr < rows and 0 <= nc < columns else 0.0
        return jnp.where(edge, beyond, rolled[r][c])

    return at


def block_of(r, c):
    return pl.ds(8 * r, 8), pl.ds(128 * c, 128)


def read(ref, *at):
    ny, nz = ref.shape[-2:]
    return [[ref[(*at, *block_of(r, c))] for c in range(nz // 128)] for r in range(ny // 8)]


def strains_of(here, before, after):
    vx, vy, vz = here
    vx_y, vx_z = shifted(vx, 0, 1), shifted(vx, 1, 1)
    vy_y, vy_z = shifted(vy, 0, -1), shifted(vy, 1, 1)
    vz_y, vz_z = shifted(vz, 0, 1), shifted(vz, 1, -1)

    def at(r, c):
        x, y, z = vx[r][c], vy[r][c], vz[r][c]
        exx = x if before is None else x - before(r, c)
        eyy = y - vy_y(r, c)
        ezz = z - vz_z(r, c)
        dy = -y if after is None else after[0](r, c) - y
        dz = -z if after is None else after[1](r, c) - z
        exy = (vx_y(r, c) - x) + dy
        exz = (vx_z(r, c) - x) + dz
        eyz = (vy_z(r, c) - y) + (vz_y(r, c) - z)
        return exx, eyy, ezz, exy, exz, eyz

    return at


def kernel(
    tiles,
    offsets,
    sources,
    params,
    adjoint,
    snapshots,
    residuals,
    receivers,
    out,
    offset,
    source_at,
    window,
    state,
    snaps,
    resid,
    recs,
    inject,
    fields,
    coef,
    grad,
    gwin,
    fromp,
    sumbuf,
    landed,
    mine,
    maxima,
    local_sem,
    p_send,
    p_recv,
    g_send,
    g_recv,
    m_send,
    m_recv,
):
    me = lax.axis_index("tile")
    core = lax.rem(me, 2)
    xbit = lax.rem(lax.div(me, 2), 2)
    partner = me + 1 - 2 * core
    far = me + 3 * (2 * core - 1)
    xn = me + 2 - 4 * xbit
    zf = me + 4 - 8 * xbit
    zr = me - 4 + 8 * xbit
    dg = me - 2 + 4 * xbit
    nx = state.shape[1]
    nf, slab = params.shape[:2]
    ny, nz = state.shape[2], state.shape[3]

    barrier = pltpu.get_barrier_semaphore()

    @pl.loop(1, tiles)
    def _(d):
        pl.semaphore_signal(
            barrier, inc=1, device_id={"tile": lax.rem(me + d, tiles)}, device_id_type=MESH
        )

    own_copy = pltpu.make_async_copy(params, window.at[REACH], local_sem.at[0])
    state_copy = pltpu.make_async_copy(adjoint.at[0, 0], state, local_sem.at[1])
    snap_copy = pltpu.make_async_copy(snapshots.at[0, 0], snaps, local_sem.at[2])
    resid_copy = pltpu.make_async_copy(residuals, resid, local_sem.at[3])
    recs_copy = pltpu.make_async_copy(receivers, recs, local_sem.at[4])
    offset_copy = pltpu.make_async_copy(offsets, offset, local_sem.at[5])
    source_copy = pltpu.make_async_copy(sources, source_at, local_sem.at[6])
    for copy in (recs_copy, resid_copy, snap_copy, own_copy, state_copy, offset_copy, source_copy):
        copy.start()
    pl.semaphore_wait(barrier, tiles - 1)

    def push(src, dst, send, recv, to):
        return pltpu.make_async_remote_copy(
            src_ref=src,
            dst_ref=dst,
            send_sem=send,
            recv_sem=recv,
            device_id={"tile": to},
            device_id_type=MESH,
        )

    def when_in(t, fn):
        pl.when(jnp.logical_and(t >= 0, t < tiles))(fn)

    slot_x = 5 - 4 * xbit
    slot_z = 1 + 4 * xbit
    to_core = 2 * core - 1

    chunks = [pl.ds(0, 1), pl.ds(1, 2), pl.ds(3, 2)]
    passed = pl.ds(0, 3)

    def send_x(k):
        block = window.at[slot_z, chunks[k]]
        return push(params.at[chunks[k]], block, p_send.at[0], p_recv.at[k], xn)

    send_own = push(params, window.at[2 + 2 * core], p_send.at[1], p_recv.at[10], partner)
    send_far = push(params, window.at[6 - 6 * core], p_send.at[2], p_recv.at[11], far)
    send_dg = push(
        params.at[chunks[2]], window.at[slot_x, chunks[2]], p_send.at[6], p_recv.at[5], dg
    )
    send_x(0).start()
    send_x(1).start()
    when_in(far, send_far.start)
    when_in(dg, send_dg.start)
    send_x(2).start()
    send_own.start()

    def on_z(k):
        block = window.at[slot_x, chunks[k]]
        return push(block, window.at[slot_z, chunks[k]], p_send.at[3], p_recv.at[3 + k], zf)

    def relay_x(k):
        block = window.at[slot_x, chunks[k]]
        there = window.at[slot_x + to_core, chunks[k]]
        return push(block, there, p_send.at[4], p_recv.at[12], partner)

    def relay_z(k):
        block = window.at[slot_z, chunks[k]]
        there = window.at[slot_z + to_core, chunks[k]]
        return push(block, there, p_send.at[5], p_recv.at[13], partner)

    def got(block, sem):
        push(block, block, p_send.at[0], sem, partner).wait_recv()

    def gone(block, sem):
        push(block, block, sem, p_recv.at[0], partner).wait_send()

    recs_copy.wait()
    resid_copy.wait()
    snap_copy.wait()
    cells = recs[...]
    lanes = cells.shape[1]
    rows = nx * ny
    blocks = [(r, c) for r in range(ny // 8) for c in range(nz // 128)]

    def pass_x(k):
        got(window.at[slot_x, chunks[k]], p_recv.at[k])
        if k < 2:
            when_in(zf, on_z(k).start)
        relay_x(k).start()

    def pass_z(k):
        got(window.at[slot_z, chunks[k]], p_recv.at[3 + k])
        relay_z(k).start()

    @pl.loop(0, STEPS)
    def _(s):
        @pl.when(s == 3)
        def _():
            pass_x(0)

        @pl.when(s == 5)
        def _():
            pass_x(1)

        def velocity(i):
            planes = []
            for c in range(3):
                u = snaps[s, c, i].astype(jnp.float32)
                fields[s, 7 + c, i] = u
                planes.append(
                    [[u[r : r + 8, k : k + 128] for k in range(0, nz, 128)] for r in range(0, ny, 8)]
                )
            return planes

        def picker(plane):
            return lambda r, c: plane[r][c]

        before, here = None, velocity(0)
        for i in range(nx):
            after = velocity(i + 1) if i + 1 < nx else None
            strains = strains_of(
                here,
                None if before is None else picker(before[0]),
                None if after is None else [picker(after[1]), picker(after[2])],
            )
            for r, c in blocks:
                fxx, fyy, fzz, fxy, fxz, fyz = strains(r, c)
                trace = fxx + fyy + fzz
                for k, value in enumerate((fxx, fyy, fzz, 0.5 * fxy, fxz, fyz, trace)):
                    fields[(s, k, i, *block_of(r, c))] = value
            before, here = here, after

        row_hit = lax.broadcasted_iota(jnp.int32, (rows, lanes), 0) == lax.div(cells, nz)
        col_hit = lax.broadcasted_iota(jnp.int32, (nz, lanes), 0) == lax.rem(cells, nz)
        columns = jnp.where(col_hit, 1.0, 0.0).astype(jnp.bfloat16)
        rest = resid[s]
        left = []
        for part in range(3):
            piece = rest.astype(jnp.bfloat16).astype(jnp.float32)
            rest = rest - piece
            left.append(jnp.where(row_hit, piece, 0.0).astype(jnp.bfloat16))
        terms = lax.dot_general(
            jnp.concatenate(left, axis=0),
            columns,
            (((1,), (1,)), ((), ())),
            preferred_element_type=jnp.float32,
        )
        total = terms[:rows] + (terms[rows : 2 * rows] + terms[2 * rows :])
        inject[s] = total.reshape(nx, ny, nz)

    pass_x(2)
    for k in range(3):
        when_in(zr, functools.partial(pass_z, k))
    got(window.at[4 - 2 * core], p_recv.at[10])
    when_in(far, lambda: got(window.at[6 * core], p_recv.at[11]))
    got(window.at[slot_x - to_core], p_recv.at[12])
    when_in(zr, lambda: got(window.at[slot_z - to_core], p_recv.at[13]))
    own_copy.wait()
    state_copy.wait()

    offset_copy.wait()
    source_copy.wait()
    rel = jnp.clip(offset[0] - me + REACH, 0, REACH)
    for j in range(APER):
        b, c11, c13, c33, c44 = [window[rel + j, f] for f in range(5)]
        here = slice(j * slab, (j + 1) * slab)
        coef[0, here] = STEP_H * b
        coef[1, here] = STEP_H * c13
        coef[2, here] = STEP_H * (c11 - c13)
        coef[3, here] = STEP_H * (c33 - c13)
        coef[4, here] = STEP_H * c44
        coef[5, here] = (0.5 * STEP_H) * (c11 - c13)

    grad[...] = jnp.zeros_like(grad)

    @pl.loop(0, STEPS)
    def _(s):
        def velocity(i):
            sxy, sxz, syy, syz, szz = [read(state, k, i) for k in (6, 7, 4, 8, 5)]
            sxy_y, sxz_z = shifted(sxy, 0, -1), shifted(sxz, 1, -1)
            syy_y, syz_z = shifted(syy, 0, 1), shifted(syz, 1, -1)
            syz_y, szz_z = shifted(syz, 0, -1), shifted(szz, 1, 1)
            for r, c in blocks:
                at = block_of(r, c)
                hb = coef[(0, i, *at)]
                sxx = state[(3, i, *at)]
                xy, xz, yy, yz, zz = [f[r][c] for f in (sxy, sxz, syy, syz, szz)]
                dxx = state[(3, i + 1, *at)] - sxx if i + 1 < nx else -sxx
                dxy = xy - state[(6, i - 1, *at)] if i > 0 else xy
                dxz = xz - state[(7, i - 1, *at)] if i > 0 else xz
                ax = dxx + ((xy - sxy_y(r, c)) + (xz - sxz_z(r, c)))
                ay = dxy + ((syy_y(r, c) - yy) + (yz - syz_z(r, c)))
                az = dxz + ((yz - syz_y(r, c)) + (szz_z(r, c) - zz))
                state[(0, i, *at)] += hb * ax
                state[(1, i, *at)] += hb * ay
                state[(2, i, *at)] = (state[(2, i, *at)] + inject[(s, i, *at)]) + hb * az

        def stress(i):
            here = [read(state, k, i) for k in range(3)]

            def picker(k, plane):
                return lambda r, c: state[(k, plane, *block_of(r, c))]

            strains = strains_of(
                here,
                picker(0, i - 1) if i > 0 else None,
                [picker(1, i + 1), picker(2, i + 1)] if i + 1 < nx else None,
            )
            for r, c in blocks:
                at = block_of(r, c)
                vx, vy, vz = [v[r][c] for v in here]
                exx, eyy, ezz, exy, exz, eyz = strains(r, c)
                h13, d11, d33, h44, h66 = [coef[(k, i, *at)] for k in range(1, 6)]
                trace = exx + eyy + ezz
                common = h13 * trace
                state[(3, i, *at)] += common + d11 * exx
                state[(4, i, *at)] += common + d11 * eyy
                state[(5, i, *at)] += common + d33 * ezz
                state[(6, i, *at)] += h66 * exy
                state[(7, i, *at)] += h44 * exz
                state[(8, i, *at)] += h44 * eyz
                fxx, fyy, fzz, fxy, fxz, fyz, ftrace, ux, uy, uz = [
                    fields[(s, k, i, *at)] for k in range(10)
                ]
                grad[(0, i, *at)] += vx * ux + vy * uy + vz * uz
                grad[(1, i, *at)] += exx * fxx + eyy * fyy + exy * fxy
                grad[(2, i, *at)] += trace * ftrace
                grad[(3, i, *at)] += ezz * fzz
                grad[(4, i, *at)] += exz * fxz + eyz * fyz

        velocity(0)
        for i in range(nx):
            if i + 1 < nx:
                velocity(i + 1)
            stress(i)

    source = source_at[0, 0]
    sx = lax.div(source, ny * nz)
    sy = lax.rem(lax.div(source, nz), ny)
    sz = lax.rem(source, nz)
    dy = lax.broadcasted_iota(jnp.int32, (ny, nz), 0) - sy
    dz = lax.broadcasted_iota(jnp.int32, (ny, nz), 1) - sz
    flat = dy * dy + dz * dz
    for i in range(nx):
        dx = i - sx
        d2 = (flat + dx * dx).astype(jnp.float32)
        weight = d2 / (d2 + float(MUTE * MUTE))
        k11, k33 = grad[1, i], grad[3, i]
        grad[2, i] = (grad[2, i] - k11 - k33) * weight
        grad[1, i] = k11 * weight
        grad[3, i] = k33 * weight
        grad[0, i] = grad[0, i] * weight
        grad[4, i] = grad[4, i] * weight

    def place(pos):
        j = pos - rel
        ok = jnp.logical_and(j >= 0, j < APER)
        start = slab * jnp.clip(j, 0, APER - 1)
        for f in range(5):
            for k in range(slab):
                gwin[pos, f, k] = jnp.where(ok, grad[f, start + k], 0.0)

    def pair_z(k):
        block = gwin.at[slot_z - to_core, chunks[k]]
        return push(block, fromp.at[0, chunks[k]], g_send.at[0], g_recv.at[10 + k], partner)

    pair_x = push(gwin.at[slot_x - to_core], fromp.at[1], g_send.at[1], g_recv.at[13], partner)
    pair_own = push(gwin.at[REACH - to_core], fromp.at[2], g_send.at[2], g_recv.at[20], partner)
    to_far = push(gwin.at[6 * core], landed.at[2], g_send.at[5], g_recv.at[21], far)

    def to_z(k):
        block = sumbuf.at[0, chunks[k]]
        return push(block, landed.at[0, chunks[k]], g_send.at[3], g_recv.at[3 + k], zr)

    to_dg = push(
        sumbuf.at[0, chunks[2]], landed.at[0, chunks[2]], g_send.at[6], g_recv.at[5], dg
    )

    def to_x(k):
        block = sumbuf.at[1, chunks[k]]
        return push(block, landed.at[1, chunks[k]], g_send.at[4], g_recv.at[k], xn)

    place(slot_z - to_core)
    for k in range(3):
        pair_z(k).start()
    place(slot_x - to_core)
    pair_x.start()
    place(slot_z)
    place(6 * core)
    for k in range(3):
        pair_z(k).wait_recv()
        sumbuf[0, chunks[k]] = gwin[slot_z, chunks[k]] + fromp[0, chunks[k]]
        when_in(zr, to_z(k).start if k < 2 else to_dg.start)
        if k == 1:
            when_in(far, to_far.start)
    place(REACH - to_core)
    pair_own.start()
    place(slot_x)
    place(REACH)
    pair_x.wait_recv()
    sumbuf[1] = gwin[slot_x] + fromp[1]
    to_x(2).start()
    for k in range(2):

        def join(k=k):
            got(landed.at[0, chunks[k]], g_recv.at[3 + k])
            sumbuf[1, chunks[k]] += landed[0, chunks[k]]

        when_in(zf, join)
        to_x(k).start()
    pair_own.wait_recv()
    out[...] = gwin[REACH] + fromp[2]

    def join_far():
        got(landed.at[2], g_recv.at[21])
        out[...] += landed[2]

    def join_dg():
        got(landed.at[0, chunks[2]], g_recv.at[5])
        out[chunks[2]] += landed[0, chunks[2]]

    when_in(far, join_far)
    when_in(zr, join_dg)
    for k in (2, 0, 1):
        got(landed.at[1, chunks[k]], g_recv.at[k])

    lane = lax.broadcasted_iota(jnp.int32, (1, 128), 1)
    row = jnp.zeros((1, 128), jnp.float32)
    for f in range(nf):
        total = out[f] + landed[1, f]
        out[f] = total
        biggest = jnp.max(jnp.abs(total), axis=(0, 1, 2), keepdims=True)[0]
        row = jnp.where(lane == f, biggest, row)
    mine[...] = row

    def max_copy(d):
        to = lax.rem(me + d, tiles)
        return push(mine, maxima.at[d - 1], m_send.at[0], m_recv.at[0], to)

    @pl.loop(1, tiles)
    def _(d):
        max_copy(d).start()

    gone(params, p_send.at[0])
    send_own.wait_send()
    when_in(far, send_far.wait_send)
    when_in(zf, lambda: gone(window.at[slot_x, passed], p_send.at[3]))
    gone(window.at[slot_x], p_send.at[4])
    when_in(zr, lambda: gone(window.at[slot_z], p_send.at[5]))
    gone(fromp.at[0], g_send.at[0])
    pair_x.wait_send()
    pair_own.wait_send()
    when_in(far, to_far.wait_send)
    when_in(zr, lambda: gone(sumbuf.at[0, passed], g_send.at[3]))
    when_in(zr, to_dg.wait_send)
    when_in(dg, send_dg.wait_send)
    gone(sumbuf.at[1], g_send.at[4])

    got(maxima, m_recv.at[0])
    scale = 1.0 / (jnp.maximum(jnp.max(maxima[...], axis=0), row) + EPSILON)
    for f in range(nf):
        out[f] = out[f] * jnp.sum(jnp.where(lane == f, scale, 0.0), axis=1, keepdims=True)
    gone(maxima, m_send.at[0])


def on_device(params, adjoint_state, snapshots, residuals, receivers, sources, offsets):
    tiles = lax.axis_size("tile")
    grid = adjoint_state.shape[3:]
    slab_shape = params.shape
    f32 = jnp.float32
    hbm = pl.BlockSpec(memory_space=pltpu.HBM)
    vmem = pl.BlockSpec(memory_space=pltpu.VMEM)
    dma = pltpu.SemaphoreType.DMA
    rows = jnp.transpose(residuals[0], (1, 0, 2))
    return pl.pallas_call(
        functools.partial(kernel, tiles),
        out_shape=jax.ShapeDtypeStruct(slab_shape, f32),
        in_specs=[hbm, hbm, hbm, hbm, hbm, hbm, hbm],
        out_specs=vmem,
        scratch_shapes=[
            pltpu.SMEM(offsets.shape, jnp.int32),
            pltpu.SMEM(sources.shape, jnp.int32),
            pltpu.VMEM((SPAN,) + slab_shape, f32),
            pltpu.VMEM((9,) + grid, f32),
            pltpu.VMEM((STEPS, 3) + grid, jnp.bfloat16),
            pltpu.VMEM(rows.shape, f32),
            pltpu.VMEM(receivers.shape[1:], jnp.int32),
            pltpu.VMEM((STEPS,) + grid, f32),
            pltpu.VMEM((STEPS, 10) + grid, f32),
            pltpu.VMEM((6,) + grid, f32),
            pltpu.VMEM((5,) + grid, f32),
            pltpu.VMEM((SPAN,) + slab_shape, f32),
            pltpu.VMEM((3,) + slab_shape, f32),
            pltpu.VMEM((2,) + slab_shape, f32),
            pltpu.VMEM((3,) + slab_shape, f32),
            pltpu.VMEM((1, 128), f32),
            pltpu.VMEM((tiles - 1, 1, 128), f32),
            dma((8,)),
            dma((7,)),
            dma((14,)),
            dma((7,)),
            dma((22,)),
            dma((1,)),
            dma((1,)),
        ],
        compiler_params=pltpu.CompilerParams(
            collective_id=0, has_side_effects=True, vmem_limit_bytes=56 * 1024 * 1024
        ),
    )(offsets, sources, params, adjoint_state, snapshots, rows, receivers[0])


def solution(mesh):
    placed = (
        P("groups", "tile", None, None),
        P("tile", "groups", None, None, None, None),
        P("tile", "groups", None, None, None, None, None),
        P("tile", "groups", None, None),
        P("tile", "groups", None),
        P("tile", "groups"),
        P("tile"),
    )
    return jax.shard_map(
        on_device,
        mesh=mesh,
        in_specs=placed,
        out_specs=P("groups", "tile", None, None),
        check_vma=False,
    )
```

```python
import functools

import jax
import jax.numpy as jnp
from jax import lax
from jax.experimental import pallas as pl
from jax.experimental.pallas import tpu as pltpu
from jax.sharding import PartitionSpec as P

STEPS = 6
APER = 4
REACH = 3
MUTE = 4
SPAN = 2 * REACH + 1

STEP_H = 0.2
EPSILON = 1e-06
MESH = pl.DeviceIdType.MESH


def shifted(blocks, axis, by):
    rows, columns = len(blocks), len(blocks[0])
    size = blocks[0][0].shape[axis]
    place = lax.broadcasted_iota(jnp.int32, blocks[0][0].shape, axis)
    edge = place == (size - 1 if by == 1 else 0)
    turn = size - 1 if by == 1 else 1
    rolled = [[pltpu.roll(b, turn, axis) for b in row] for row in blocks]

    def at(r, c):
        nr, nc = (r + by, c) if axis == 0 else (r, c + by)
        beyond = rolled[nr][nc] if 0 <= nr < rows and 0 <= nc < columns else 0.0
        return jnp.where(edge, beyond, rolled[r][c])

    return at


def block_of(r, c):
    return pl.ds(8 * r, 8), pl.ds(128 * c, 128)


def read(ref, *at):
    ny, nz = ref.shape[-2:]
    return [[ref[(*at, *block_of(r, c))] for c in range(nz // 128)] for r in range(ny // 8)]


def strains_of(here, before, after):
    vx, vy, vz = here
    vx_y, vx_z = shifted(vx, 0, 1), shifted(vx, 1, 1)
    vy_y, vy_z = shifted(vy, 0, -1), shifted(vy, 1, 1)
    vz_y, vz_z = shifted(vz, 0, 1), shifted(vz, 1, -1)

    def at(r, c):
        x, y, z = vx[r][c], vy[r][c], vz[r][c]
        exx = x if before is None else x - before(r, c)
        eyy = y - vy_y(r, c)
        ezz = z - vz_z(r, c)
        dy = -y if after is None else after[0](r, c) - y
        dz = -z if after is None else after[1](r, c) - z
        exy = (vx_y(r, c) - x) + dy
        exz = (vx_z(r, c) - x) + dz
        eyz = (vy_z(r, c) - y) + (vz_y(r, c) - z)
        return exx, eyy, ezz, exy, exz, eyz

    return at


def kernel(
    tiles,
    offsets,
    sources,
    params,
    adjoint,
    snapshots,
    residuals,
    receivers,
    out,
    offset,
    source_at,
    window,
    state,
    snaps,
    resid,
    recs,
    inject,
    fields,
    coef,
    grad,
    gwin,
    fromp,
    sumbuf,
    landed,
    mine,
    maxima,
    local_sem,
    p_send,
    p_recv,
    g_send,
    g_recv,
    m_send,
    m_recv,
):
    me = lax.axis_index("tile")
    core = lax.rem(me, 2)
    xbit = lax.rem(lax.div(me, 2), 2)
    partner = me + 1 - 2 * core
    far = me + 3 * (2 * core - 1)
    xn = me + 2 - 4 * xbit
    zf = me + 4 - 8 * xbit
    zr = me - 4 + 8 * xbit
    dg = me - 2 + 4 * xbit
    nx = state.shape[1]
    nf, slab = params.shape[:2]
    ny, nz = state.shape[2], state.shape[3]

    barrier = pltpu.get_barrier_semaphore()

    @pl.loop(1, tiles)
    def _(d):
        pl.semaphore_signal(
            barrier, inc=1, device_id={"tile": lax.rem(me + d, tiles)}, device_id_type=MESH
        )

    own_copy = pltpu.make_async_copy(params, window.at[REACH], local_sem.at[0])
    state_copy = pltpu.make_async_copy(adjoint.at[0, 0], state, local_sem.at[1])
    snap_copy = pltpu.make_async_copy(snapshots.at[0, 0], snaps, local_sem.at[2])
    resid_copy = pltpu.make_async_copy(residuals, resid, local_sem.at[3])
    recs_copy = pltpu.make_async_copy(receivers, recs, local_sem.at[4])
    offset_copy = pltpu.make_async_copy(offsets, offset, local_sem.at[5])
    source_copy = pltpu.make_async_copy(sources, source_at, local_sem.at[6])
    for copy in (recs_copy, resid_copy, snap_copy, own_copy, state_copy, offset_copy, source_copy):
        copy.start()
    pl.semaphore_wait(barrier, tiles - 1)

    def push(src, dst, send, recv, to):
        return pltpu.make_async_remote_copy(
            src_ref=src,
            dst_ref=dst,
            send_sem=send,
            recv_sem=recv,
            device_id={"tile": to},
            device_id_type=MESH,
        )

    def when_in(t, fn):
        pl.when(jnp.logical_and(t >= 0, t < tiles))(fn)

    slot_x = 5 - 4 * xbit
    slot_z = 1 + 4 * xbit
    to_core = 2 * core - 1

    chunks = [pl.ds(0, 2), pl.ds(2, 3)]
    passed = pl.ds(0, 2)

    def send_x(k):
        block = window.at[slot_z, chunks[k]]
        return push(params.at[chunks[k]], block, p_send.at[0], p_recv.at[k], xn)

    send_own = push(params, window.at[2 + 2 * core], p_send.at[1], p_recv.at[10], partner)
    send_far = push(params, window.at[6 - 6 * core], p_send.at[2], p_recv.at[11], far)
    send_dg = push(
        params.at[chunks[1]], window.at[slot_x, chunks[1]], p_send.at[6], p_recv.at[4], dg
    )
    send_x(0).start()
    when_in(far, send_far.start)
    when_in(dg, send_dg.start)
    send_x(1).start()
    send_own.start()

    def on_z(k):
        block = window.at[slot_x, chunks[k]]
        return push(block, window.at[slot_z, chunks[k]], p_send.at[3], p_recv.at[3 + k], zf)

    def relay_x(k):
        block = window.at[slot_x, chunks[k]]
        there = window.at[slot_x + to_core, chunks[k]]
        return push(block, there, p_send.at[4], p_recv.at[12], partner)

    def relay_z(k):
        block = window.at[slot_z, chunks[k]]
        there = window.at[slot_z + to_core, chunks[k]]
        return push(block, there, p_send.at[5], p_recv.at[13], partner)

    def got(block, sem):
        push(block, block, p_send.at[0], sem, partner).wait_recv()

    def gone(block, sem):
        push(block, block, sem, p_recv.at[0], partner).wait_send()

    recs_copy.wait()
    resid_copy.wait()
    snap_copy.wait()
    cells = recs[...]
    lanes = cells.shape[1]
    rows = nx * ny
    blocks = [(r, c) for r in range(ny // 8) for c in range(nz // 128)]

    def pass_x(k):
        got(window.at[slot_x, chunks[k]], p_recv.at[k])
        if k == 0:
            when_in(zf, on_z(k).start)
        relay_x(k).start()

    def pass_z(k):
        got(window.at[slot_z, chunks[k]], p_recv.at[3 + k])
        relay_z(k).start()

    @pl.loop(0, STEPS)
    def _(s):
        @pl.when(s == 3)
        def _():
            pass_x(0)

        def velocity(i):
            planes = []
            for c in range(3):
                u = snaps[s, c, i].astype(jnp.float32)
                fields[s, 7 + c, i] = u
                planes.append(
                    [[u[r : r + 8, k : k + 128] for k in range(0, nz, 128)] for r in range(0, ny, 8)]
                )
            return planes

        def picker(plane):
            return lambda r, c: plane[r][c]

        before, here = None, velocity(0)
        for i in range(nx):
            after = velocity(i + 1) if i + 1 < nx else None
            strains = strains_of(
                here,
                None if before is None else picker(before[0]),
                None if after is None else [picker(after[1]), picker(after[2])],
            )
            for r, c in blocks:
                fxx, fyy, fzz, fxy, fxz, fyz = strains(r, c)
                trace = fxx + fyy + fzz
                for k, value in enumerate((fxx, fyy, fzz, 0.5 * fxy, fxz, fyz, trace)):
                    fields[(s, k, i, *block_of(r, c))] = value
            before, here = here, after

        row_hit = lax.broadcasted_iota(jnp.int32, (rows, lanes), 0) == lax.div(cells, nz)
        col_hit = lax.broadcasted_iota(jnp.int32, (nz, lanes), 0) == lax.rem(cells, nz)
        columns = jnp.where(col_hit, 1.0, 0.0).astype(jnp.bfloat16)
        rest = resid[s]
        left = []
        for part in range(3):
            piece = rest.astype(jnp.bfloat16).astype(jnp.float32)
            rest = rest - piece
            left.append(jnp.where(row_hit, piece, 0.0).astype(jnp.bfloat16))
        terms = lax.dot_general(
            jnp.concatenate(left, axis=0),
            columns,
            (((1,), (1,)), ((), ())),
            preferred_element_type=jnp.float32,
        )
        total = terms[:rows] + (terms[rows : 2 * rows] + terms[2 * rows :])
        inject[s] = total.reshape(nx, ny, nz)

    pass_x(1)
    for k in range(2):
        when_in(zr, functools.partial(pass_z, k))
    got(window.at[4 - 2 * core], p_recv.at[10])
    when_in(far, lambda: got(window.at[6 * core], p_recv.at[11]))
    got(window.at[slot_x - to_core], p_recv.at[12])
    when_in(zr, lambda: got(window.at[slot_z - to_core], p_recv.at[13]))
    own_copy.wait()
    state_copy.wait()

    offset_copy.wait()
    source_copy.wait()
    rel = jnp.clip(offset[0] - me + REACH, 0, REACH)
    for j in range(APER):
        b, c11, c13, c33, c44 = [window[rel + j, f] for f in range(5)]
        here = slice(j * slab, (j + 1) * slab)
        coef[0, here] = STEP_H * b
        coef[1, here] = STEP_H * c13
        coef[2, here] = STEP_H * (c11 - c13)
        coef[3, here] = STEP_H * (c33 - c13)
        coef[4, here] = STEP_H * c44
        coef[5, here] = (0.5 * STEP_H) * (c11 - c13)

    grad[...] = jnp.zeros_like(grad)

    @pl.loop(0, STEPS)
    def _(s):
        def velocity(i):
            sxy, sxz, syy, syz, szz = [read(state, k, i) for k in (6, 7, 4, 8, 5)]
            sxy_y, sxz_z = shifted(sxy, 0, -1), shifted(sxz, 1, -1)
            syy_y, syz_z = shifted(syy, 0, 1), shifted(syz, 1, -1)
            syz_y, szz_z = shifted(syz, 0, -1), shifted(szz, 1, 1)
            for r, c in blocks:
                at = block_of(r, c)
                hb = coef[(0, i, *at)]
                sxx = state[(3, i, *at)]
                xy, xz, yy, yz, zz = [f[r][c] for f in (sxy, sxz, syy, syz, szz)]
                dxx = state[(3, i + 1, *at)] - sxx if i + 1 < nx else -sxx
                dxy = xy - state[(6, i - 1, *at)] if i > 0 else xy
                dxz = xz - state[(7, i - 1, *at)] if i > 0 else xz
                ax = dxx + ((xy - sxy_y(r, c)) + (xz - sxz_z(r, c)))
                ay = dxy + ((syy_y(r, c) - yy) + (yz - syz_z(r, c)))
                az = dxz + ((yz - syz_y(r, c)) + (szz_z(r, c) - zz))
                state[(0, i, *at)] += hb * ax
                state[(1, i, *at)] += hb * ay
                state[(2, i, *at)] = (state[(2, i, *at)] + inject[(s, i, *at)]) + hb * az

        def stress(i):
            here = [read(state, k, i) for k in range(3)]

            def picker(k, plane):
                return lambda r, c: state[(k, plane, *block_of(r, c))]

            strains = strains_of(
                here,
                picker(0, i - 1) if i > 0 else None,
                [picker(1, i + 1), picker(2, i + 1)] if i + 1 < nx else None,
            )
            for r, c in blocks:
                at = block_of(r, c)
                vx, vy, vz = [v[r][c] for v in here]
                exx, eyy, ezz, exy, exz, eyz = strains(r, c)
                h13, d11, d33, h44, h66 = [coef[(k, i, *at)] for k in range(1, 6)]
                trace = exx + eyy + ezz
                common = h13 * trace
                state[(3, i, *at)] += common + d11 * exx
                state[(4, i, *at)] += common + d11 * eyy
                state[(5, i, *at)] += common + d33 * ezz
                state[(6, i, *at)] += h66 * exy
                state[(7, i, *at)] += h44 * exz
                state[(8, i, *at)] += h44 * eyz
                fxx, fyy, fzz, fxy, fxz, fyz, ftrace, ux, uy, uz = [
                    fields[(s, k, i, *at)] for k in range(10)
                ]
                grad[(0, i, *at)] += vx * ux + vy * uy + vz * uz
                grad[(1, i, *at)] += exx * fxx + eyy * fyy + exy * fxy
                grad[(2, i, *at)] += trace * ftrace
                grad[(3, i, *at)] += ezz * fzz
                grad[(4, i, *at)] += exz * fxz + eyz * fyz

        velocity(0)
        for i in range(nx):
            if i + 1 < nx:
                velocity(i + 1)
            stress(i)

    source = source_at[0, 0]
    sx = lax.div(source, ny * nz)
    sy = lax.rem(lax.div(source, nz), ny)
    sz = lax.rem(source, nz)
    dy = lax.broadcasted_iota(jnp.int32, (ny, nz), 0) - sy
    dz = lax.broadcasted_iota(jnp.int32, (ny, nz), 1) - sz
    flat = dy * dy + dz * dz
    for i in range(nx):
        dx = i - sx
        d2 = (flat + dx * dx).astype(jnp.float32)
        weight = d2 / (d2 + float(MUTE * MUTE))
        k11, k33 = grad[1, i], grad[3, i]
        grad[2, i] = (grad[2, i] - k11 - k33) * weight
        grad[1, i] = k11 * weight
        grad[3, i] = k33 * weight
        grad[0, i] = grad[0, i] * weight
        grad[4, i] = grad[4, i] * weight

    def place(pos):
        j = pos - rel
        ok = jnp.logical_and(j >= 0, j < APER)
        start = slab * jnp.clip(j, 0, APER - 1)
        for f in range(5):
            for k in range(slab):
                gwin[pos, f, k] = jnp.where(ok, grad[f, start + k], 0.0)

    def pair_z(k):
        block = gwin.at[slot_z - to_core, chunks[k]]
        return push(block, fromp.at[0, chunks[k]], g_send.at[0], g_recv.at[10 + k], partner)

    pair_x = push(gwin.at[slot_x - to_core], fromp.at[1], g_send.at[1], g_recv.at[13], partner)
    pair_own = push(gwin.at[REACH - to_core], fromp.at[2], g_send.at[2], g_recv.at[20], partner)
    to_far = push(gwin.at[6 * core], landed.at[2], g_send.at[5], g_recv.at[21], far)

    def to_z(k):
        block = sumbuf.at[0, chunks[k]]
        return push(block, landed.at[0, chunks[k]], g_send.at[3], g_recv.at[3 + k], zr)

    to_dg = push(
        sumbuf.at[0, chunks[1]], landed.at[0, chunks[1]], g_send.at[6], g_recv.at[4], dg
    )

    def to_x(k):
        block = sumbuf.at[1, chunks[k]]
        return push(block, landed.at[1, chunks[k]], g_send.at[4], g_recv.at[k], xn)

    place(slot_z - to_core)
    for k in range(2):
        pair_z(k).start()
    place(slot_x - to_core)
    pair_x.start()
    place(slot_z)
    place(6 * core)
    for k in range(2):
        pair_z(k).wait_recv()
        sumbuf[0, chunks[k]] = gwin[slot_z, chunks[k]] + fromp[0, chunks[k]]
        when_in(zr, to_z(k).start if k == 0 else to_dg.start)
        if k == 0:
            when_in(far, to_far.start)
    place(REACH - to_core)
    pair_own.start()
    place(slot_x)
    place(REACH)
    pair_x.wait_recv()
    sumbuf[1] = gwin[slot_x] + fromp[1]
    to_x(1).start()
    for k in range(1):

        def join(k=k):
            got(landed.at[0, chunks[k]], g_recv.at[3 + k])
            sumbuf[1, chunks[k]] += landed[0, chunks[k]]

        when_in(zf, join)
        to_x(k).start()
    pair_own.wait_recv()
    out[...] = gwin[REACH] + fromp[2]

    def join_far():
        got(landed.at[2], g_recv.at[21])
        out[...] += landed[2]

    def join_dg():
        got(landed.at[0, chunks[1]], g_recv.at[4])
        out[chunks[1]] += landed[0, chunks[1]]

    when_in(far, join_far)
    when_in(zr, join_dg)
    for k in (1, 0):
        got(landed.at[1, chunks[k]], g_recv.at[k])

    lane = lax.broadcasted_iota(jnp.int32, (1, 128), 1)
    row = jnp.zeros((1, 128), jnp.float32)
    for f in range(nf):
        total = out[f] + landed[1, f]
        out[f] = total
        biggest = jnp.max(jnp.abs(total), axis=(0, 1, 2), keepdims=True)[0]
        row = jnp.where(lane == f, biggest, row)
    mine[...] = row

    def max_copy(d):
        to = lax.rem(me + d, tiles)
        return push(mine, maxima.at[d - 1], m_send.at[0], m_recv.at[0], to)

    @pl.loop(1, tiles)
    def _(d):
        max_copy(d).start()

    gone(params, p_send.at[0])
    send_own.wait_send()
    when_in(far, send_far.wait_send)
    when_in(zf, lambda: gone(window.at[slot_x, passed], p_send.at[3]))
    gone(window.at[slot_x], p_send.at[4])
    when_in(zr, lambda: gone(window.at[slot_z], p_send.at[5]))
    gone(fromp.at[0], g_send.at[0])
    pair_x.wait_send()
    pair_own.wait_send()
    when_in(far, to_far.wait_send)
    when_in(zr, lambda: gone(sumbuf.at[0, passed], g_send.at[3]))
    when_in(zr, to_dg.wait_send)
    when_in(dg, send_dg.wait_send)
    gone(sumbuf.at[1], g_send.at[4])

    got(maxima, m_recv.at[0])
    scale = 1.0 / (jnp.maximum(jnp.max(maxima[...], axis=0), row) + EPSILON)
    for f in range(nf):
        out[f] = out[f] * jnp.sum(jnp.where(lane == f, scale, 0.0), axis=1, keepdims=True)
    gone(maxima, m_send.at[0])


def on_device(params, adjoint_state, snapshots, residuals, receivers, sources, offsets):
    tiles = lax.axis_size("tile")
    grid = adjoint_state.shape[3:]
    slab_shape = params.shape
    f32 = jnp.float32
    hbm = pl.BlockSpec(memory_space=pltpu.HBM)
    vmem = pl.BlockSpec(memory_space=pltpu.VMEM)
    dma = pltpu.SemaphoreType.DMA
    rows = jnp.transpose(residuals[0], (1, 0, 2))
    return pl.pallas_call(
        functools.partial(kernel, tiles),
        out_shape=jax.ShapeDtypeStruct(slab_shape, f32),
        in_specs=[hbm, hbm, hbm, hbm, hbm, hbm, hbm],
        out_specs=vmem,
        scratch_shapes=[
            pltpu.SMEM(offsets.shape, jnp.int32),
            pltpu.SMEM(sources.shape, jnp.int32),
            pltpu.VMEM((SPAN,) + slab_shape, f32),
            pltpu.VMEM((9,) + grid, f32),
            pltpu.VMEM((STEPS, 3) + grid, jnp.bfloat16),
            pltpu.VMEM(rows.shape, f32),
            pltpu.VMEM(receivers.shape[1:], jnp.int32),
            pltpu.VMEM((STEPS,) + grid, f32),
            pltpu.VMEM((STEPS, 10) + grid, f32),
            pltpu.VMEM((6,) + grid, f32),
            pltpu.VMEM((5,) + grid, f32),
            pltpu.VMEM((SPAN,) + slab_shape, f32),
            pltpu.VMEM((3,) + slab_shape, f32),
            pltpu.VMEM((2,) + slab_shape, f32),
            pltpu.VMEM((3,) + slab_shape, f32),
            pltpu.VMEM((1, 128), f32),
            pltpu.VMEM((tiles - 1, 1, 128), f32),
            dma((8,)),
            dma((7,)),
            dma((14,)),
            dma((7,)),
            dma((22,)),
            dma((1,)),
            dma((1,)),
        ],
        compiler_params=pltpu.CompilerParams(
            collective_id=0, has_side_effects=True, vmem_limit_bytes=56 * 1024 * 1024
        ),
    )(offsets, sources, params, adjoint_state, snapshots, rows, receivers[0])


def solution(mesh):
    placed = (
        P("groups", "tile", None, None),
        P("tile", "groups", None, None, None, None),
        P("tile", "groups", None, None, None, None, None),
        P("tile", "groups", None, None),
        P("tile", "groups", None),
        P("tile", "groups"),
        P("tile"),
    )
    return jax.shard_map(
        on_device,
        mesh=mesh,
        in_specs=placed,
        out_specs=P("groups", "tile", None, None),
        check_vma=False,
    )
```
